128 devices in a mesh: fsdp: 16 (over y, x), exp: 8 (over z, core).
Axes of the slice: x: 4, y: 4, z: 4, core: 2. Of those that a mesh axis runs over, the one named last changes fastest.
Arguments:
- tokens: bfloat16 [16384, 3584], P(('fsdp', 'exp')), may hold values from -6 to 6
- grad_out: bfloat16 [16384, 3584], P(('fsdp', 'exp')), may hold values from -6 to 6
- route_probs: bfloat16 [16384, 2], P(('fsdp', 'exp')), may hold values from 0.19921875 to 1
- expert_ids: int32 [16384, 2], P(('fsdp', 'exp')), may hold values from 0 to 7, all different within a row; in each aligned block of 128 rows (0 to 127, 128 to 255, ...) at most 34 rows name the same one
- saved_pre: bfloat16 [8, 4352, 2, 2432], P('exp', None, None, 'fsdp'), may hold values from -6 to 6
- expert_weights: bfloat16 [8, 3584, 3, 2432], P('exp', None, None, 'fsdp'), may hold values from -0.09375 to 0.09375
Outputs:
- grad_tokens: bfloat16 [16384, 3584], P(('fsdp', 'exp'))
- expert_grad: bfloat16 [8, 3584, 3, 2432], P('exp', None, None, 'fsdp')
The draws below stay inside these ranges and needn't reach their ends.
Inputs may be any that keep to these rules, and one draw needn't show every extreme that they name: `expert_ids`: A token's two experts differ. Among the 128 tokens of one device no expert is named more than 34 times, and in every draw some device names some expert exactly 34 times.
All inputs are finite; a program needn't handle non-finite values.
Results may differ from the reference program's by a relative error of at most 0.02.
Values may be sent and summed in bfloat16 or wider, within the bound.
A program may use at most 320 MiB of HBM per device.

```python
import math
import jax
import jax.numpy as jnp
import numpy as np
from jax import lax

D = 3584
HE = 2432
TOK_DEV = 128
EXPERTS = 8
CAP = 34
SLOTS = 4352
TOKENS = 16384
N_FSDP = 16
N_EXP = 8


def level_of(own_key, extent, split, least, top_value):
    level = 1.0
    for position, shards_of in split:
        heights = jax.random.uniform(jax.random.fold_in(jax.random.fold_in(own_key, 6), position), (shards_of,), jnp.float32, least / len(split), top_value / len(split))
        level = level * jnp.repeat(jnp.exp(heights), extent[position] // shards_of).reshape((-1,) + (1,) * (len(extent) - 1 - position))
    return level


def routed_block(key, own, number, rows, count, top, bound, slope):
    order = jax.random.permutation(key, count)
    packed, common = portions_of(count, rows * top, bound, slope, True), portions_of(count, rows * top, bound, slope, False)
    places = jnp.arange(count)

    def named(tallies, offset_by):
        used = int((tallies > 0).sum())
        fixed = max(1, used // 4)
        passed = fixed + (places - fixed + offset_by * (used - fixed)) % max(1, count - fixed)
        return jnp.zeros((count,), jnp.int32).at[order[jnp.where(places < fixed, places, passed)]].set(jnp.asarray(tallies, jnp.int32))

    tallies = jnp.where(number % 4 == 0, named(packed, number // 4), named(common, number - number // 4 - 1))
    mixed = jax.random.permutation(jax.random.fold_in(own, 3), count)
    donor, taker = mixed[0:count // 2 * 2:2], mixed[1:count // 2 * 2:2]
    margin = jnp.minimum(tallies[donor] - 1, bound - tallies[taker]) // 2
    margin = jnp.where((donor == order[0]) | (taker == order[0]) | (tallies[taker] == 0), 0, jnp.maximum(margin, 0))
    passed = jax.random.randint(jax.random.fold_in(own, 4), (count // 2,), 0, 1 << 20) % (margin + 1)
    tallies = tallies.at[donor].add(-passed).at[taker].add(passed)
    labels = jnp.searchsorted(jnp.cumsum(tallies), jnp.arange(rows * top), side="right").astype(jnp.int32)
    grid = labels.reshape(top, rows).T
    grid = grid[jax.random.permutation(jax.random.fold_in(own, 1), rows)]
    offset_by = jax.random.randint(jax.random.fold_in(own, 2), (rows, 1), 0, top)
    return jnp.take_along_axis(grid, (jnp.arange(top)[None, :] + offset_by) % top, axis=1)


def portions_of(amount, total, bound, slope, full):
    loads = [(1 << 20) // math.isqrt(grade ** slope) + 1 for grade in range(1, amount + 1)]
    largest = bound if full else min(bound, max(-(-total // amount), total * loads[0] // sum(loads)))
    least = 1 if total - largest >= amount - 1 else 0
    counts, rest = [largest] + [least] * (amount - 1), total - largest - least * (amount - 1)
    while rest > 0:
        candidates = [i for i in range(1, amount) if counts[i] < largest] or [i for i in range(1, amount) if counts[i] < bound]
        mass, left = sum([loads[i] for i in candidates]), rest
        for i in candidates:
            addition = min(bound - counts[i], max(1, left * loads[i] // mass), rest)
            counts[i] = counts[i] + addition
            rest = rest - addition
    return np.array(counts)


def scatter_about(own_key, extent, spread, reach, split=(), kind=jnp.bfloat16):
    factor_of = level_of(own_key, extent, split, -0.22, 0.18) if split else 1.0
    entries = jax.random.normal(own_key, extent, jnp.float32) * spread * factor_of
    return jnp.minimum(jnp.maximum(entries, -reach), reach).astype(kind)


def setup_inputs(seed: int = 0) -> dict:
    key_list = jax.random.split(jax.random.key(seed), 7)
    tokens = scatter_about(key_list[0], (TOKENS, D), 1.0, 6.0, ((0, 128),))
    grad_out = scatter_about(key_list[1], (TOKENS, D), 1.0, 6.0, ((0, 128),))
    route_probs = jnp.clip(0.19921875 + 0.80078125 * jax.random.uniform(key_list[2], (TOKENS, 2), jnp.float32) ** level_of(key_list[2], (TOKENS, 2), ((0, 128),), -0.2, 0.2), 0.19921875, 1.0).astype(jnp.bfloat16)
    expert_ids_keys = jax.random.split(jax.random.fold_in(key_list[3], 1), TOKENS // TOK_DEV)
    expert_ids_turns = jax.random.permutation(jax.random.fold_in(key_list[3], 3), TOKENS // TOK_DEV)
    expert_ids = jax.vmap(lambda own, number: routed_block(jax.random.fold_in(key_list[3], 2), own, number, TOK_DEV, EXPERTS, 2, CAP, 2))(expert_ids_keys, expert_ids_turns).reshape((TOKENS, 2))
    saved_pre = scatter_about(key_list[4], (EXPERTS, SLOTS, 2, HE), 1.5, 6.0, ((0, 8), (3, 16)))
    expert_weights = scatter_about(key_list[5], (EXPERTS, D, 3, HE), D ** -0.5, 0.09375, ((0, 8), (3, 16)))
    return dict(tokens=tokens, grad_out=grad_out, route_probs=route_probs, expert_ids=expert_ids, saved_pre=saved_pre, expert_weights=expert_weights)


def swiglu_back(gate_pre, up_pre, back):
    sig = jax.nn.sigmoid(gate_pre)
    act = gate_pre * sig
    hidden = act * up_pre
    d_gate = back * up_pre * sig * (1.0 + gate_pre * (1.0 - sig))
    d_up = back * act
    return jnp.concatenate([d_gate, d_up], 1).astype(jnp.bfloat16), hidden


def reference(tokens, grad_out, route_probs, expert_ids, saved_pre, expert_weights):
    devices = N_FSDP * N_EXP
    slots_all = devices * CAP
    share = HE // N_FSDP
    ids_dev = expert_ids.reshape(devices, 2 * TOK_DEV)
    onehot = (ids_dev[:, :, None] == jnp.arange(EXPERTS, dtype=jnp.int32)[None, None, :]).astype(jnp.int32)
    before = jnp.cumsum(onehot, axis=1) - onehot
    slot = jnp.sum(before * onehot, axis=-1)
    device_row = jnp.arange(devices, dtype=jnp.int32)[:, None]
    dest = (device_row * EXPERTS + ids_dev) * CAP + slot
    assign = jnp.arange(devices * 2 * TOK_DEV, dtype=jnp.int32)
    table = jnp.full((devices * EXPERTS * CAP,), -1, jnp.int32).at[dest.reshape(-1)].set(assign)
    table = table.reshape(devices, EXPERTS, CAP).transpose(1, 0, 2).reshape(EXPERTS, slots_all)
    flat_probs = route_probs.reshape(-1).astype(jnp.float32)

    def one_expert(total, item):
        which, weights, pre = item
        mask = which >= 0
        index = jnp.where(mask, which, 0).astype(jnp.int32)
        tok = index // 2
        xs = jnp.where(mask[:, None], tokens[tok], jnp.zeros((), jnp.bfloat16)).astype(jnp.bfloat16)
        dys = jnp.where(mask[:, None], grad_out[tok], jnp.zeros((), jnp.bfloat16)).astype(jnp.bfloat16)
        ps = jnp.where(mask, flat_probs[index], jnp.zeros((), jnp.float32))
        gate_pre = pre[:, 0, :].astype(jnp.float32)
        up_pre = pre[:, 1, :].astype(jnp.float32)
        back_e = ps[:, None] * jnp.dot(dys, weights[:, 2, :], preferred_element_type=jnp.float32)
        grads_e, hidden_e = swiglu_back(gate_pre, up_pre, back_e)
        scaled = (ps[:, None] * hidden_e).astype(jnp.bfloat16)
        pieces = grads_e.reshape(slots_all, 2, N_FSDP, share).astype(jnp.float32)
        proj = weights[:, :2, :].reshape(D, 2, N_FSDP, share).astype(jnp.float32)
        part_dx = jnp.einsum('skfh,dkfh->fsd', pieces, proj).astype(jnp.bfloat16)
        part_dx = lax.optimization_barrier(part_dx).astype(jnp.float32)
        slot_dx = jnp.sum(part_dx, axis=0).astype(jnp.bfloat16)
        first = jnp.dot(xs.T, grads_e, preferred_element_type=jnp.float32)
        last = jnp.dot(dys.T, scaled, preferred_element_type=jnp.float32)
        grad = jnp.concatenate([first.reshape(D, 2, HE), last[:, None, :]], 1).astype(jnp.bfloat16)
        added = jnp.where(mask[:, None], slot_dx.astype(jnp.float32), jnp.zeros((), jnp.float32))
        total = total.at[tok].add(added)
        return total, grad

    start = jnp.zeros((TOKENS, D), jnp.float32)
    moe_dx, expert_grad = lax.scan(one_expert, start, (table, expert_weights, saved_pre))
    return moe_dx.astype(jnp.bfloat16), expert_grad
```

```python
import functools

import jax
import jax.numpy as jnp
import numpy as np
from jax import lax
from jax.experimental import pallas as pl
from jax.experimental.pallas import tpu as pltpu
from jax.sharding import PartitionSpec as P

MESH = pl.DeviceIdType.MESH
BF16 = jnp.bfloat16
F32 = jnp.float32
SIDE = 4
N_COPIES = 80


def round_up(value, unit):
    return -(-value // unit) * unit


def chunk_of(width):
    return 512 if width % 512 == 0 else 128


def dot(left, right, dims):
    return lax.dot_general(left, right, (dims, ((), ())), preferred_element_type=F32)


def rows_of(start, size):
    return pl.ds(pl.multiple_of(start, 16), size)


def cols_of(start, size):
    return pl.ds(pl.multiple_of(start, 128), size)


def kernel(
    cap,
    capp,
    ids_ref,
    probs_ref,
    tok_ref,
    gout_ref,
    pack_ref,
    unpack_ref,
    w_hbm,
    w2_hbm,
    pre_hbm,
    gt_ref,
    dw_hbm,
    g_buf,
    x_buf,
    w13,
    w2,
    pre,
    dgt,
    dg,
    sct,
    acc,
    asend,
    arecv,
    dxr,
    sxt,
    send_sem,
    recv_sem,
    local_sem,
    credit_a,
    credit_b,
    credit_z,
):
    f = lax.axis_index("fsdp")
    e = lax.axis_index("exp")
    experts = lax.axis_size("exp")
    q, p = f // SIDE, f % SIDE
    tokens, width = tok_ref.shape
    half = width // 2
    low, high = pl.ds(0, half), pl.ds(half, half)
    nc = chunk_of(width)
    steps = width // nc
    slots = experts * capp
    rb = experts * cap
    rows = SIDE * rb
    rp = g_buf.shape[0]
    h2 = w13.shape[0] // SIDE
    h = h2 // 2
    hp = w2.shape[0] // SIDE
    shift = (rows * q) % 128

    def dev_p(d):
        return (SIDE * q + (p + d) % SIDE, e)

    def dev_q(d):
        return (SIDE * ((q + d) % SIDE) + p, e)

    def dev_e(d):
        return (f, (e + d) % experts)

    count = [0]

    def rcopy(src, dst, dev):
        i = count[0]
        count[0] += 1
        c = pltpu.make_async_remote_copy(
            src_ref=src,
            dst_ref=dst,
            send_sem=send_sem.at[i],
            recv_sem=recv_sem.at[i],
            device_id=dev,
            device_id_type=MESH,
        )
        c.start()
        return c

    barrier = pltpu.get_barrier_semaphore()
    peers = [dev_p(1), dev_p(3), dev_q(1), dev_q(2), dev_q(3)]
    peers += [dev_e(d) for d in range(1, experts)]
    for dev in peers:
        pl.semaphore_signal(barrier, inc=1, device_id=dev, device_id_type=MESH)
    pl.semaphore_wait(barrier, len(peers))

    def pre_cols(to):
        return cols_of((rows * to) // 128 * 128, rp)

    my_pre = pl.ds(pl.multiple_of(q * rp, 128), rp)
    w13_src = w_hbm.at[pl.ds(0, h2)]

    def ring_start(src, buf, off, pos, dev):
        mine = buf.at[off(pos)]
        return [rcopy(src, mine, dev(1)), rcopy(src, mine, dev(3))]

    def ring_forward(first, buf, off, pos, dev):
        first[0].wait_recv()
        part = buf.at[off((pos + 3) % SIDE), low]
        up = rcopy(part, part, dev(1))
        first[1].wait_recv()
        part = buf.at[off((pos + 1) % SIDE), high]
        down = rcopy(part, part, dev(3))
        return [up, down]

    def wait_recv(copies):
        for c in copies:
            c.wait_recv()

    def wait_send(copies):
        for c in copies:
            c.wait_send()

    w2_off = lambda j: rows_of(hp * j, hp)
    w13_off = lambda j: rows_of(h2 * j, h2)
    row_off = lambda b: rows_of(shift + rb * b, rb)

    w2_copies = ring_start(w2_hbm, w2, w2_off, q, dev_q)
    pre_copies = [
        rcopy(pre_hbm.at[:, pre_cols((q + d) % SIDE)], pre.at[:, my_pre], dev_q(d))
        for d in (1, 2, 3)
    ]
    w13_copies = ring_start(w13_src, w13, w13_off, q, dev_q)
    local = [
        pltpu.make_async_copy(w2_hbm, w2.at[w2_off(q)], local_sem.at[0]),
        pltpu.make_async_copy(pre_hbm.at[:, pre_cols(q)], pre.at[:, my_pre], local_sem.at[1]),
        pltpu.make_async_copy(w13_src, w13.at[w13_off(q)], local_sem.at[2]),
    ]
    for c in local:
        c.start()

    ids = ids_ref[...]
    probs = probs_ref[...].astype(F32)
    kinds = lax.broadcasted_iota(jnp.int32, (experts, tokens), 0)
    hit = [(kinds == ids[k : k + 1, :]).astype(F32) for k in (0, 1)]
    earlier = (
        lax.broadcasted_iota(jnp.int32, (tokens, tokens), 0)
        < lax.broadcasted_iota(jnp.int32, (tokens, tokens), 1)
    ).astype(BF16)
    before = dot((hit[0] + hit[1]).astype(BF16), earlier, ((1,), (0,)))
    place = lax.broadcasted_iota(jnp.int32, (slots, tokens), 0)
    chosen = []
    for k in (0, 1):
        slot = jnp.sum(before * hit[k], axis=0, keepdims=True).astype(jnp.int32)
        chosen.append((place == ids[k : k + 1, :] * capp + slot).astype(F32))
    pick = chosen[0] + chosen[1]
    sxt[...] = jnp.transpose(pick).astype(BF16)
    pick_g = (chosen[0] * probs[0:1, :] + chosen[1] * probs[1:2, :]).astype(BF16)
    pick_x = pick.astype(BF16)

    def exchange(base, copies_from, dst_base):
        copies = []
        for d in range(1, experts):
            src = copies_from.at[rows_of(base + capp * ((e + d) % experts), capp)]
            dst = arecv.at[rows_of(dst_base + capp * e, capp)]
            copies.append(rcopy(src, dst, dev_e(d)))
        return copies

    def dispatch(base, matrix, source):
        def body(n, _):
            cols = cols_of(n * nc, nc)
            asend[pl.ds(base, slots), cols] = dot(
                matrix, source[:, cols], ((1,), (0,))
            ).astype(BF16)
            return 0

        lax.fori_loop(0, steps, body, 0)
        return exchange(base, asend, base)

    g_sent = dispatch(0, pick_g, gout_ref)
    x_sent = dispatch(slots, pick_x, tok_ref)

    blank = rows_of(rows * (1 - q % 2), rp - rows)
    g_buf[blank, :] = jnp.zeros((rp - rows, width), BF16)
    x_buf[blank, :] = jnp.zeros((rp - rows, width), BF16)

    def compact(base, buf):
        own = rows_of(base + capp * e, capp)
        arecv[own, :] = asend[own, :]

        def body(n, _):
            cols = cols_of(n * nc, nc)
            buf[row_off(p), cols] = dot(
                pack_ref[...], arecv[pl.ds(base, slots), cols], ((1,), (0,))
            ).astype(BF16)
            return 0

        lax.fori_loop(0, steps, body, 0)

    wait_recv(g_sent)
    compact(0, g_buf)
    g_copies = ring_start(g_buf.at[row_off(p)], g_buf, row_off, p, dev_p)
    for d in range(1, experts):
        pl.semaphore_signal(credit_z, inc=1, device_id=dev_e(d), device_id_type=MESH)
    wait_recv(x_sent)
    compact(slots, x_buf)
    x_copies = ring_start(x_buf.at[row_off(p)], x_buf, row_off, p, dev_p)

    w2_copies += ring_forward(w2_copies, w2, w2_off, q, dev_q)
    g_copies += ring_forward(g_copies, g_buf, row_off, p, dev_p)
    for c in local:
        c.wait()
    wait_recv(w2_copies[2:])
    w13_copies += ring_forward(w13_copies, w13, w13_off, q, dev_q)
    wait_recv(g_copies[2:])

    acc[...] = jnp.zeros_like(acc)

    def back_step(n, _):
        cols = cols_of(n * nc, nc)
        acc[...] += dot(w2[:, cols], g_buf[:, cols], ((1,), (1,)))
        return 0

    lax.fori_loop(0, steps, back_step, 0)
    x_copies += ring_forward(x_copies, x_buf, row_off, p, dev_p)
    wait_recv(pre_copies)

    def activate(i, _):
        j, c = i // (rp // 128), i % (rp // 128)
        lanes = cols_of(c * 128, 128)
        saved = pre[:, cols_of(j * rp + c * 128, 128)].astype(F32)
        back = acc[rows_of(hp * j, hp), lanes][:h]
        a, b = saved[:h], saved[h:]
        sig = jax.nn.sigmoid(a)
        act = a * sig
        d_gate = back * b * sig * (1.0 + a * (1.0 - sig))
        d_up = back * act
        dgt[rows_of(h2 * j, h2), lanes] = jnp.concatenate([d_gate, d_up], 0).astype(BF16)
        scaled = jnp.concatenate([act * b, jnp.zeros((hp - h, 128), F32)], 0)
        sct[rows_of(hp * j, hp), lanes] = scaled.astype(BF16)
        return 0

    lax.fori_loop(0, SIDE * (rp // 128), activate, 0)

    wait_send(w2_copies)
    for d in (1, 3):
        pl.semaphore_signal(credit_a, inc=1, device_id=dev_q(d), device_id_type=MESH)

    def send_far(part, off, pos, dst, dev):
        far = off((pos + 2) % SIDE)
        return [
            rcopy(part.at[far, low], dst.at[:, low], dev(1)),
            rcopy(part.at[far, high], dst.at[:, high], dev(3)),
        ]

    def send_near_direct(part, off, pos, dst, dev):
        return [
            rcopy(part.at[off((pos + 1) % SIDE), high], dst[0].at[:, high], dev(1)),
            rcopy(part.at[off((pos + 3) % SIDE), low], dst[1].at[:, low], dev(3)),
        ]

    def add_into(part, where, others, start, size):
        ac = 256 if half % 256 == 0 else 128

        def body(n, _):
            cols = cols_of(start + n * ac, ac)
            total = part[where, cols].astype(F32)
            for ref in others:
                total = total + ref[:, cols].astype(F32)
            part[where, cols] = total.astype(BF16)
            return 0

        lax.fori_loop(0, size // ac, body, 0)

    def send_near_added(far, part, off, pos, got, dst, dev):
        far[0].wait_recv()
        where = off((pos + 1) % SIDE)
        add_into(part, where, [got], 0, half)
        up = rcopy(part.at[where, low], dst[0].at[:, low], dev(1))
        far[1].wait_recv()
        where = off((pos + 3) % SIDE)
        add_into(part, where, [got], half, half)
        down = rcopy(part.at[where, high], dst[1].at[:, high], dev(3))
        return [up, down]

    wait_send(g_sent)
    wait_send(x_sent)

    def dw2_step(n, _):
        cols = cols_of(n * nc, nc)
        asend[pl.ds(0, SIDE * hp), cols] = dot(sct[...], g_buf[:, cols], ((1,), (0,))).astype(BF16)
        return 0

    lax.fori_loop(0, steps, dw2_step, 0)
    pl.semaphore_wait(credit_a, 2)
    dw2_near = [w2.at[pl.ds(hp, hp)], w2.at[pl.ds(2 * hp, hp)]]
    dw2_far_got = w2.at[pl.ds(0, hp)]
    dw2_far = send_far(asend, w2_off, q, dw2_far_got, dev_q)
    dw2_mid = send_near_direct(asend, w2_off, q, dw2_near, dev_q)

    def flip(c, _):
        lanes = cols_of(c * 128, 128)
        dg[rows_of(c * 128, 128), :] = jnp.transpose(dgt[:, lanes])
        return 0

    lax.fori_loop(0, rp // 128, flip, 0)

    wait_send(g_copies)
    wait_recv(w13_copies[2:])
    dx_off = lambda b: rows_of(rb * b, rb)

    def dx_block(d):
        b = (p + d) % SIDE

        def body(n, _):
            cols = cols_of(n * nc, nc)
            g_buf[dx_off(b), cols] = dot(dg[row_off(b), :], w13[:, cols], ((1,), (0,))).astype(BF16)
            return 0

        lax.fori_loop(0, steps, body, 0)

    dx_far_got = dxr.at[pl.ds(0, rb)]
    dx_near = [dxr.at[pl.ds(rb, rb)], dxr.at[pl.ds(2 * rb, rb)]]
    dx_block(2)
    dx_far = send_far(g_buf, dx_off, p, dx_far_got, dev_p)
    dx_block(1)
    dx_block(3)
    dx_mid = send_near_direct(g_buf, dx_off, p, dx_near, dev_p)
    dx_block(0)
    dw2_mid += send_near_added(dw2_far, asend, w2_off, q, dw2_far_got, dw2_near, dev_q)
    dx_mid += send_near_added(dx_far, g_buf, dx_off, p, dx_far_got, dx_near, dev_p)

    wait_send(w13_copies)
    wait_recv(x_copies[2:])

    def dw13_block(d):
        j = (q + d) % SIDE

        def body(n, _):
            cols = cols_of(n * nc, nc)
            w13[w13_off(j), cols] = dot(
                dgt[w13_off(j), :], x_buf[:, cols], ((1,), (0,))
            ).astype(BF16)
            return 0

        lax.fori_loop(0, steps, body, 0)

    dw13_far_got = pre.at[:, pl.ds(0, width)]
    dw13_near = [x_buf.at[pl.ds(0, h2)], x_buf.at[pl.ds(h2, h2)]]
    dw13_block(2)
    dw13_far = send_far(w13, w13_off, q, dw13_far_got, dev_q)
    dw13_block(1)
    dw13_block(3)
    dw13_block(0)
    wait_send(x_copies)
    for d in (1, 3):
        pl.semaphore_signal(credit_b, inc=1, device_id=dev_q(d), device_id_type=MESH)
    pl.semaphore_wait(credit_b, 2)
    dw13_mid = send_near_direct(w13, w13_off, q, dw13_near, dev_q)
    dw13_mid += send_near_added(dw13_far, w13, w13_off, q, dw13_far_got, dw13_near, dev_q)

    wait_recv(dx_mid)
    add_into(g_buf, dx_off(p), dx_near, 0, width)
    ret_base = slots

    def expand(n, _):
        cols = cols_of(n * nc, nc)
        arecv[pl.ds(ret_base, slots), cols] = dot(
            unpack_ref[...], g_buf[dx_off(p), cols], ((1,), (0,))
        ).astype(BF16)
        return 0

    lax.fori_loop(0, steps, expand, 0)
    pl.semaphore_wait(credit_z, experts - 1)
    ret = exchange(ret_base, arecv, 0)
    arecv[rows_of(capp * e, capp), :] = arecv[rows_of(ret_base + capp * e, capp), :]

    wait_recv(dw2_mid)
    add_into(asend, w2_off(q), dw2_near, 0, width)
    out2 = pltpu.make_async_copy(
        asend.at[w2_off(q)], dw_hbm.at[pl.ds(h2, hp)], local_sem.at[3]
    )
    out2.start()

    wait_recv(ret)

    def combine(n, _):
        cols = cols_of(n * nc, nc)
        gt_ref[:, cols] = dot(sxt[...], arecv[pl.ds(0, slots), cols], ((1,), (0,))).astype(BF16)
        return 0

    lax.fori_loop(0, steps, combine, 0)

    wait_recv(dw13_mid)
    add_into(w13, w13_off(q), dw13_near, 0, width)
    out13 = pltpu.make_async_copy(
        w13.at[w13_off(q)], dw_hbm.at[pl.ds(0, h2)], local_sem.at[4]
    )
    out13.start()

    wait_send(pre_copies)
    wait_send(dw2_far + dw2_mid + dx_far + dx_mid + dw13_far + dw13_mid + ret)
    out2.wait()
    out13.wait()


def on_device(tokens, grad_out, route_probs, expert_ids, saved_pre, expert_weights):
    rows, width = tokens.shape
    experts = lax.axis_size("exp")
    cap = 17 * rows // (8 * experts)
    capp = round_up(cap, 16)
    slots = experts * capp
    rb = experts * cap
    hidden = expert_weights.shape[3]
    hp = round_up(hidden, 16)
    rp = round_up(SIDE * rb + 64, 128)
    w = jnp.transpose(expert_weights[0], (1, 2, 0)).reshape(3 * hidden, width)
    w2 = jnp.pad(w[2 * hidden :], ((0, hp - hidden), (0, 0)))
    pre = jnp.transpose(saved_pre[0], (1, 2, 0)).reshape(2 * hidden, saved_pre.shape[1])
    at = np.arange(rb)
    pack = np.zeros((rb, slots), np.float32)
    pack[at, at // cap * capp + at % cap] = 1
    vmem = pl.BlockSpec(memory_space=pltpu.VMEM)
    hbm = pl.BlockSpec(memory_space=pl.ANY)
    gt, dw = pl.pallas_call(
        functools.partial(kernel, cap, capp),
        out_shape=(
            jax.ShapeDtypeStruct((rows, width), BF16),
            jax.ShapeDtypeStruct((2 * hidden + hp, width), BF16),
        ),
        in_specs=[vmem] * 6 + [hbm] * 3,
        out_specs=(vmem, hbm),
        scratch_shapes=[
            pltpu.VMEM((rp, width), BF16),
            pltpu.VMEM((rp, width), BF16),
            pltpu.VMEM((SIDE * 2 * hidden, width), BF16),
            pltpu.VMEM((SIDE * hp, width), BF16),
            pltpu.VMEM((2 * hidden, SIDE * rp), BF16),
            pltpu.VMEM((SIDE * 2 * hidden, rp), BF16),
            pltpu.VMEM((rp, SIDE * 2 * hidden), BF16),
            pltpu.VMEM((SIDE * hp, rp), BF16),
            pltpu.VMEM((SIDE * hp, rp), F32),
            pltpu.VMEM((max(2 * slots, SIDE * hp), width), BF16),
            pltpu.VMEM((2 * slots, width), BF16),
            pltpu.VMEM((3 * rb, width), BF16),
            pltpu.VMEM((rows, slots), BF16),
            pltpu.SemaphoreType.DMA((N_COPIES,)),
            pltpu.SemaphoreType.DMA((N_COPIES,)),
            pltpu.SemaphoreType.DMA((5,)),
            pltpu.SemaphoreType.REGULAR,
            pltpu.SemaphoreType.REGULAR,
            pltpu.SemaphoreType.REGULAR,
        ],
        compiler_params=pltpu.CompilerParams(
            collective_id=0, has_side_effects=True, vmem_limit_bytes=64 * 2**20
        ),
        name="experts_backward",
    )(
        expert_ids.T,
        route_probs.T,
        tokens,
        grad_out,
        jnp.asarray(pack, BF16),
        jnp.asarray(pack.T, BF16),
        w,
        w2,
        pre,
    )
    grad = dw[: 3 * hidden].reshape(3, hidden, width)
    return gt, jnp.transpose(grad, (2, 0, 1))[None]


def solution(mesh):
    in_specs = (
        P(("fsdp", "exp"), None),
        P(("fsdp", "exp"), None),
        P(("fsdp", "exp"), None),
        P(("fsdp", "exp"), None),
        P("exp", None, None, "fsdp"),
        P("exp", None, None, "fsdp"),
    )
    out_specs = (P(("fsdp", "exp"), None), P("exp", None, None, "fsdp"))
    return jax.shard_map(
        on_device, mesh=mesh, in_specs=in_specs, out_specs=out_specs, check_vma=False
    )
```

```python
import functools

import jax
import jax.numpy as jnp
import numpy as np
from jax import lax
from jax.experimental import pallas as pl
from jax.experimental.pallas import tpu as pltpu
from jax.sharding import PartitionSpec as P

MESH = pl.DeviceIdType.MESH
BF16 = jnp.bfloat16
F32 = jnp.float32
SIDE = 4
N_COPIES = 128


def round_up(value, unit):
    return -(-value // unit) * unit


def chunk_of(width):
    return 512 if width % 512 == 0 else 128


def dot(left, right, dims):
    return lax.dot_general(left, right, (dims, ((), ())), preferred_element_type=F32)


def rows_of(start, size):
    return pl.ds(pl.multiple_of(start, 16), size)


def cols_of(start, size):
    return pl.ds(pl.multiple_of(start, 128), size)


def kernel(
    cap,
    pieces,
    ids_ref,
    probs_ref,
    gout_ref,
    tok_ref,
    lmap_ref,
    fold_ref,
    unfold_ref,
    w_hbm,
    w2_hbm,
    pre_hbm,
    gt_ref,
    dw_hbm,
    g_buf,
    x_buf,
    w13,
    w2,
    pre,
    dgt,
    dg,
    sct,
    acc,
    stage,
    gmain,
    dxr,
    gext,
    gext_got,
    rext,
    rext_got,
    xext,
    xext_got,
    home,
    home_ext,
    send_sem,
    recv_sem,
    local_sem,
    credit_a,
    credit_b,
    credit_z,
):
    f = lax.axis_index("fsdp")
    e = lax.axis_index("exp")
    experts = lax.axis_size("exp")
    core = e % 2
    q = core * (f % SIDE) + (1 - core) * (f // SIDE)
    p = core * (f // SIDE) + (1 - core) * (f % SIDE)
    tokens, width = gout_ref.shape
    half = width // 2
    low, high = pl.ds(0, half), pl.ds(half, half)
    nc = chunk_of(width)
    steps = width // nc
    mb = cap // 16 * 16
    xb = cap - mb
    main = experts * mb
    rb = experts * cap
    rows = SIDE * rb
    rp = g_buf.shape[0]
    h2 = w13.shape[0] // SIDE
    h = h2 // 2
    hp = w2.shape[0] // SIDE
    piece = width // pieces

    def dev_at(pp, qq):
        return (SIDE * (core * pp + (1 - core) * qq) + core * qq + (1 - core) * pp, e)

    def dev_p(d):
        return dev_at((p + d) % SIDE, q)

    def dev_q(d):
        return dev_at(p, (q + d) % SIDE)

    def dev_e(d):
        return (f, (e + d) % experts)

    count = [0]

    def rcopy(src, dst, dev):
        i = count[0]
        count[0] += 1
        c = pltpu.make_async_remote_copy(
            src_ref=src,
            dst_ref=dst,
            send_sem=send_sem.at[i],
            recv_sem=recv_sem.at[i],
            device_id=dev,
            device_id_type=MESH,
        )
        c.start()
        return c

    def signal(sem, devs):
        for dev in devs:
            pl.semaphore_signal(sem, inc=1, device_id=dev, device_id_type=MESH)

    barrier = pltpu.get_barrier_semaphore()
    peers = [dev_p(d) for d in (1, 2, 3)] + [dev_q(d) for d in (1, 2, 3)]
    peers += [dev_e(d) for d in range(1, experts)]
    signal(barrier, peers)
    pl.semaphore_wait(barrier, len(peers))

    def ring_start(src, buf, off, pos, dev):
        mine = buf.at[off(pos)]
        return [rcopy(src, mine, dev(1)), rcopy(src, mine, dev(3))]

    def ring_forward(first, buf, off, pos, dev):
        first[0].wait_recv()
        part = buf.at[off((pos + 3) % SIDE), low]
        up = rcopy(part, part, dev(1))
        first[1].wait_recv()
        part = buf.at[off((pos + 1) % SIDE), high]
        down = rcopy(part, part, dev(3))
        return [up, down]

    def wait_recv(copies):
        for c in copies:
            c.wait_recv()

    def wait_send(copies):
        for c in copies:
            c.wait_send()

    w2_off = lambda j: rows_of(hp * j, hp)
    w13_off = lambda j: rows_of(h2 * j, h2)
    row_off = lambda b: rows_of(rb * b, rb)
    ext_off = lambda b: rows_of(rb * b + main, 16)
    w13_src = w_hbm.at[pl.ds(0, h2)]
    my_pre = pl.ds(pl.multiple_of(q * rp, 128), rp)

    w2_copies = ring_start(w2_hbm, w2, w2_off, q, dev_q)
    strip = pre_hbm.shape[1] // 2
    local = [
        pltpu.make_async_copy(
            pre_hbm.at[:, pl.ds(i * strip, strip)],
            stage.at[pl.ds(i * h2, h2), pl.ds(0, strip)],
            local_sem.at[i],
        )
        for i in (0, 1)
    ]
    local += [
        pltpu.make_async_copy(w2_hbm, w2.at[w2_off(q)], local_sem.at[2]),
        pltpu.make_async_copy(w13_src, w13.at[w13_off(q)], local_sem.at[3]),
    ]
    for c in local:
        c.start()

    ids = ids_ref[...]
    probs = probs_ref[...].astype(F32)
    kinds = lax.broadcasted_iota(jnp.int32, (experts, tokens), 0)
    hit = [(kinds == ids[k : k + 1, :]).astype(F32) for k in (0, 1)]
    earlier = (
        lax.broadcasted_iota(jnp.int32, (tokens, tokens), 0)
        < lax.broadcasted_iota(jnp.int32, (tokens, tokens), 1)
    ).astype(F32).astype(BF16)
    before = dot((hit[0] + hit[1]).astype(BF16), earlier, ((1,), (0,)))
    at_main, at_ext = [], []
    for k in (0, 1):
        own = ids[k : k + 1, :]
        slot = jnp.sum(before * hit[k], axis=0, keepdims=True).astype(jnp.int32)
        inside = slot < mb
        at_main.append(jnp.where(inside, mb * own + slot, -4096))
        at_ext.append(jnp.where(inside, -4096, 16 * own + pieces * (slot - mb)))

    def one_hot(size, where):
        line = lax.broadcasted_iota(jnp.int32, (size, tokens), 0)
        return [(line == w).astype(F32) for w in where]

    def dispatch(source, weights, big, small):
        pick = one_hot(main, at_main)
        if weights is None:
            home[...] = jnp.transpose(pick[0] + pick[1]).astype(BF16)
            pick = (pick[0] + pick[1]).astype(BF16)
        else:
            pick = (pick[0] * weights[0:1, :] + pick[1] * weights[1:2, :]).astype(BF16)

        def pick_step(n, _):
            cols = cols_of(n * nc, nc)
            big[:, cols] = dot(pick, source[:, cols], ((1,), (0,))).astype(BF16)
            return 0

        lax.fori_loop(0, steps, pick_step, 0)
        folded = jnp.zeros((experts * 16, piece), F32)
        for j in range(pieces):
            pick = one_hot(experts * 16, [w + j for w in at_ext])
            if weights is None:
                pick = pick[0] + pick[1]
                home_ext[pl.ds(j * tokens, tokens), :] = jnp.transpose(pick).astype(BF16)
            else:
                pick = pick[0] * weights[0:1, :] + pick[1] * weights[1:2, :]
            folded += dot(pick.astype(BF16), source[:, pl.ds(j * piece, piece)], ((1,), (0,)))
        small[...] = folded.astype(BF16)

    my_slots = rows_of(rb * p + mb * e, mb)

    def exchange(big, small, buf, small_got):
        copies = []
        for d in range(1, experts):
            to = (e + d) % experts
            there = p if d % 2 == 0 else q
            copies += [
                rcopy(
                    big.at[rows_of(mb * to, mb)],
                    buf.at[rows_of(rb * there + mb * e, mb)],
                    dev_e(d),
                ),
                rcopy(small.at[rows_of(16 * to, 16)], small_got.at[rows_of(16 * e, 16)], dev_e(d)),
            ]
        buf[my_slots, :] = big[rows_of(mb * e, mb), :]
        small_got[rows_of(16 * e, 16), :] = small[rows_of(16 * e, 16), :]
        return copies

    def unfold(buf, small_got):
        for j in range(pieces):
            buf[ext_off(p), pl.ds(j * piece, piece)] = dot(
                unfold_ref[pl.ds(16 * j, 16), :], small_got[...], ((1,), (0,))
            ).astype(BF16)

    xmain = stage.at[pl.ds(2 * h2, main), pl.ds(0, width)]
    dispatch(gout_ref, probs, gmain, gext)
    g_sent = exchange(gmain, gext, g_buf, gext_got)
    dispatch(tok_ref, None, xmain, xext)
    blank = pl.ds(rows, rp - rows)
    g_buf[blank, :] = jnp.zeros((rp - rows, width), BF16)
    x_buf[blank, :] = jnp.zeros((rp - rows, width), BF16)

    local[0].wait()
    local[1].wait()
    span = rp // 3
    line = lax.broadcasted_iota(jnp.int32, (span, span), 0)
    lane = lax.broadcasted_iota(jnp.int32, (span, span), 1)

    def regroup(to, _):
        for n in range(3):
            total = jnp.zeros((h2, span), F32)
            source = lmap_ref[0:1, pl.ds(n * span, span)]
            for b in (n, n + 1):
                block = core * (SIDE * b + to) + (1 - core) * (SIDE * to + b)
                start = rb * (block % 8)
                window = stage[rows_of(block // 8 * h2, h2), cols_of(start // 128 * 128, span)]
                at = lane + (n * span - rb * b)
                match = (at >= 0) & (at < rb) & (line - start % 128 == source)
                total += dot(window, match.astype(F32).astype(BF16), ((1,), (0,)))
            dgt[rows_of(h2 * to, h2), pl.ds(n * span, span)] = total.astype(BF16)
        return 0

    lax.fori_loop(0, SIDE, regroup, 0)
    pre_copies = [
        rcopy(dgt.at[rows_of(h2 * ((q + d) % SIDE), h2)], pre.at[:, my_pre], dev_q(d))
        for d in (1, 2, 3)
    ]
    own_pre = pltpu.make_async_copy(dgt.at[rows_of(h2 * q, h2)], pre.at[:, my_pre], local_sem.at[0])
    own_pre.start()

    w13_copies = ring_start(w13_src, w13, w13_off, q, dev_q)
    w2_copies += ring_forward(w2_copies, w2, w2_off, q, dev_q)

    wait_recv(g_sent)
    unfold(g_buf, gext_got)
    g_copies = ring_start(g_buf.at[row_off(p)], g_buf, row_off, p, dev_p)

    x_sent = exchange(xmain, xext, x_buf, xext_got)
    w13_copies += ring_forward(w13_copies, w13, w13_off, q, dev_q)
    g_copies += ring_forward(g_copies, g_buf, row_off, p, dev_p)
    wait_recv(x_sent)
    unfold(x_buf, xext_got)
    x_copies = ring_start(x_buf.at[row_off(p)], x_buf, row_off, p, dev_p)

    wait_send(g_sent)
    signal(credit_z, [dev_e(d) for d in range(1, experts)])
    local[2].wait()
    local[3].wait()
    wait_recv(w2_copies[2:])
    wait_recv(g_copies[2:])

    acc[...] = jnp.zeros_like(acc)

    def back_step(n, _):
        cols = cols_of(n * nc, nc)
        acc[...] += dot(w2[:, cols], g_buf[:, cols], ((1,), (1,)))
        return 0

    lax.fori_loop(0, steps, back_step, 0)
    x_copies += ring_forward(x_copies, x_buf, row_off, p, dev_p)
    wait_recv(pre_copies)
    wait_send(pre_copies)
    own_pre.wait()

    def activate(i, _):
        j, c = i // (rp // 128), i % (rp // 128)
        lanes = cols_of(c * 128, 128)
        saved = pre[:, cols_of(j * rp + c * 128, 128)].astype(F32)
        back = acc[rows_of(hp * j, hp), lanes][:h]
        a, b = saved[:h], saved[h:]
        sig = jax.nn.sigmoid(a)
        act = a * sig
        d_gate = back * b * sig * (1.0 + a * (1.0 - sig))
        d_up = back * act
        dgt[rows_of(h2 * j, h2), lanes] = jnp.concatenate([d_gate, d_up], 0).astype(BF16)
        scaled = jnp.concatenate([act * b, jnp.zeros((hp - h, 128), F32)], 0)
        sct[rows_of(hp * j, hp), lanes] = scaled.astype(BF16)
        return 0

    lax.fori_loop(0, SIDE * (rp // 128), activate, 0)

    wait_send(w2_copies)
    signal(credit_a, [dev_q(1), dev_q(3)])

    def send_far(part, off, pos, dst, dev):
        far = off((pos + 2) % SIDE)
        return [
            rcopy(part.at[far, low], dst.at[:, low], dev(1)),
            rcopy(part.at[far, high], dst.at[:, high], dev(3)),
        ]

    def send_near_direct(part, off, pos, dst, dev):
        return [
            rcopy(part.at[off((pos + 1) % SIDE), high], dst[0].at[:, high], dev(1)),
            rcopy(part.at[off((pos + 3) % SIDE), low], dst[1].at[:, low], dev(3)),
        ]

    def add_into(part, where, others, start, size):
        ac = 256 if half % 256 == 0 else 128

        def add_step(n, _):
            cols = cols_of(start + n * ac, ac)
            total = part[where, cols].astype(F32)
            for ref in others:
                total = total + ref[:, cols].astype(F32)
            part[where, cols] = total.astype(BF16)
            return 0

        lax.fori_loop(0, size // ac, add_step, 0)

    def send_near_added(far, part, off, pos, got, dst, dev):
        far[0].wait_recv()
        where = off((pos + 1) % SIDE)
        add_into(part, where, [got], 0, half)
        up = rcopy(part.at[where, low], dst[0].at[:, low], dev(1))
        far[1].wait_recv()
        where = off((pos + 3) % SIDE)
        add_into(part, where, [got], half, half)
        down = rcopy(part.at[where, high], dst[1].at[:, high], dev(3))
        return [up, down]

    wait_send(x_sent)

    def dw2_step(n, _):
        cols = cols_of(n * nc, nc)
        stage[pl.ds(0, SIDE * hp), cols] = dot(sct[...], g_buf[:, cols], ((1,), (0,))).astype(BF16)
        return 0

    lax.fori_loop(0, steps, dw2_step, 0)
    pl.semaphore_wait(credit_a, 2)
    dw2_near = [w2.at[pl.ds(hp, hp)], w2.at[pl.ds(2 * hp, hp)]]
    dw2_far_got = w2.at[pl.ds(0, hp)]
    dw2_far = send_far(stage, w2_off, q, dw2_far_got, dev_q)
    dw2_mid = send_near_direct(stage, w2_off, q, dw2_near, dev_q)

    def flip(c, _):
        lanes = cols_of(c * 128, 128)
        dg[rows_of(c * 128, 128), :] = jnp.transpose(dgt[:, lanes])
        return 0

    lax.fori_loop(0, rp // 128, flip, 0)
    dw2_mid += send_near_added(dw2_far, stage, w2_off, q, dw2_far_got, dw2_near, dev_q)

    wait_send(g_copies)
    wait_recv(w13_copies[2:])

    def dx_block(d):
        b = (p + d) % SIDE

        def dx_step(n, _):
            cols = cols_of(n * nc, nc)
            g_buf[row_off(b), cols] = dot(dg[row_off(b), :], w13[:, cols], ((1,), (0,))).astype(BF16)
            return 0

        lax.fori_loop(0, steps, dx_step, 0)

    dx_far_got = dxr.at[pl.ds(0, rb), pl.ds(0, width)]
    dx_near = [dxr.at[pl.ds(rb * i, rb), pl.ds(0, width)] for i in (1, 2)]
    dx_block(2)
    dx_far = send_far(g_buf, row_off, p, dx_far_got, dev_p)
    dx_block(1)
    dx_block(3)
    dx_mid = send_near_direct(g_buf, row_off, p, dx_near, dev_p)
    dx_block(0)
    dx_mid += send_near_added(dx_far, g_buf, row_off, p, dx_far_got, dx_near, dev_p)

    wait_recv(x_copies[2:])
    wait_send(w13_copies)

    def dw13_block(d):
        j = (q + d) % SIDE

        def dw13_step(n, _):
            cols = cols_of(n * nc, nc)
            w13[w13_off(j), cols] = dot(
                dgt[w13_off(j), :], x_buf[:, cols], ((1,), (0,))
            ).astype(BF16)
            return 0

        lax.fori_loop(0, steps, dw13_step, 0)

    dw13_far_got = pre.at[:, pl.ds(0, width)]
    dw13_near = [x_buf.at[pl.ds(0, h2)], x_buf.at[pl.ds(h2, h2)]]
    dw13_block(2)
    dw13_far = send_far(w13, w13_off, q, dw13_far_got, dev_q)
    dw13_block(1)
    dw13_block(3)
    dw13_block(0)
    wait_send(x_copies)
    signal(credit_b, [dev_q(1), dev_q(3)])
    pl.semaphore_wait(credit_b, 2)
    dw13_mid = send_near_direct(w13, w13_off, q, dw13_near, dev_q)
    dw13_mid += send_near_added(dw13_far, w13, w13_off, q, dw13_far_got, dw13_near, dev_q)

    wait_recv(dx_mid)
    add_into(g_buf, row_off(p), dx_near, 0, width)
    folded = jnp.zeros((experts * 16, piece), F32)
    for j in range(pieces):
        folded += dot(
            fold_ref[pl.ds(j * experts * 16, experts * 16), :],
            g_buf[ext_off(p), pl.ds(j * piece, piece)],
            ((1,), (0,)),
        )
    rext[...] = folded.astype(BF16)
    pl.semaphore_wait(credit_z, experts - 1)
    ret = []
    for d in range(1, experts):
        to = (e + d) % experts
        ret.append(
            rcopy(
                g_buf.at[rows_of(rb * p + mb * to, mb)], gmain.at[rows_of(mb * e, mb)], dev_e(d)
            )
        )
        ret.append(
            rcopy(rext.at[rows_of(16 * to, 16)], rext_got.at[rows_of(16 * e, 16)], dev_e(d))
        )
    gmain[rows_of(mb * e, mb), :] = g_buf[my_slots, :]
    rext_got[rows_of(16 * e, 16), :] = rext[rows_of(16 * e, 16), :]

    wait_recv(dw2_mid)
    add_into(stage, w2_off(q), dw2_near, 0, width)
    out2 = pltpu.make_async_copy(
        stage.at[w2_off(q), pl.ds(0, width)], dw_hbm.at[pl.ds(h2, hp)], local_sem.at[0]
    )
    out2.start()

    wait_recv(ret)
    for j in range(pieces):
        cols = pl.ds(j * piece, piece)
        total = dot(home[...], gmain[:, cols], ((1,), (0,)))
        total += dot(home_ext[pl.ds(j * tokens, tokens), :], rext_got[...], ((1,), (0,)))
        gt_ref[:, cols] = total.astype(BF16)

    wait_recv(dw13_mid)
    add_into(w13, w13_off(q), dw13_near, 0, width)
    out13 = pltpu.make_async_copy(w13.at[w13_off(q)], dw_hbm.at[pl.ds(0, h2)], local_sem.at[1])
    out13.start()

    wait_send(dw2_far + dw2_mid + dx_far + dx_mid + dw13_far + dw13_mid + ret)
    out2.wait()
    out13.wait()


def on_device(tokens, grad_out, route_probs, expert_ids, saved_pre, expert_weights):
    rows, width = tokens.shape
    experts = lax.axis_size("exp")
    cap = 17 * rows // (8 * experts)
    mb = cap // 16 * 16
    xb = cap - mb
    main = experts * mb
    rb = experts * cap
    hidden = expert_weights.shape[3]
    hp = round_up(hidden, 16)
    rp = round_up(SIDE * rb + 64, 128)
    strip = saved_pre.shape[1] // 2
    pieces = max(k for k in range(1, 16 // xb + 1) if width % (128 * k) == 0)
    w = jnp.transpose(expert_weights[0], (1, 2, 0)).reshape(3 * hidden, width)
    w2 = lax.pad(w, jnp.zeros((), BF16), ((-2 * hidden, hp - hidden, 0), (0, 0, 0)))
    pre = jnp.transpose(saved_pre[0], (1, 2, 0)).reshape(2 * hidden, saved_pre.shape[1])

    at = np.arange(rb)
    in_main = at // mb * cap + at % mb
    in_ext = (at - main) // xb * cap + mb + (at - main) % xb
    lmap = np.full((8, rp), -1, np.int32)
    lmap[:, : SIDE * rb] = np.tile(np.where(at < main, in_main, in_ext), SIDE)
    ext = np.arange(16)
    unfold = np.zeros((pieces, 16, experts * 16), np.float32)
    for j in range(pieces):
        unfold[j, ext, 16 * (ext // xb) + pieces * (ext % xb) + j] = 1
    fold = unfold.transpose(0, 2, 1).reshape(pieces * experts * 16, 16)
    unfold = unfold.reshape(pieces * 16, experts * 16)

    vmem = pl.BlockSpec(memory_space=pltpu.VMEM)
    hbm = pl.BlockSpec(memory_space=pl.ANY)
    gt, dw = pl.pallas_call(
        functools.partial(kernel, cap, pieces),
        out_shape=(
            jax.ShapeDtypeStruct((rows, width), BF16),
            jax.ShapeDtypeStruct((2 * hidden + hp, width), BF16),
        ),
        in_specs=[vmem] * 7 + [hbm] * 3,
        out_specs=(vmem, hbm),
        scratch_shapes=[
            pltpu.VMEM((rp, width), BF16),
            pltpu.VMEM((rp, width), BF16),
            pltpu.VMEM((SIDE * 2 * hidden, width), BF16),
            pltpu.VMEM((SIDE * hp, width), BF16),
            pltpu.VMEM((2 * hidden, SIDE * rp), BF16),
            pltpu.VMEM((SIDE * 2 * hidden, rp), BF16),
            pltpu.VMEM((rp, SIDE * 2 * hidden), BF16),
            pltpu.VMEM((SIDE * hp, rp), BF16),
            pltpu.VMEM((SIDE * hp, rp), F32),
            pltpu.VMEM((4 * hidden + main, max(width, strip)), BF16),
            pltpu.VMEM((main, width), BF16),
            pltpu.VMEM((3 * rb, width), BF16),
            pltpu.VMEM((experts * 16, width // pieces), BF16),
            pltpu.VMEM((experts * 16, width // pieces), BF16),
            pltpu.VMEM((experts * 16, width // pieces), BF16),
            pltpu.VMEM((experts * 16, width // pieces), BF16),
            pltpu.VMEM((experts * 16, width // pieces), BF16),
            pltpu.VMEM((experts * 16, width // pieces), BF16),
            pltpu.VMEM((rows, main), BF16),
            pltpu.VMEM((pieces * rows, experts * 16), BF16),
            pltpu.SemaphoreType.DMA((N_COPIES,)),
            pltpu.SemaphoreType.DMA((N_COPIES,)),
            pltpu.SemaphoreType.DMA((5,)),
            pltpu.SemaphoreType.REGULAR,
            pltpu.SemaphoreType.REGULAR,
            pltpu.SemaphoreType.REGULAR,
        ],
        compiler_params=pltpu.CompilerParams(
            collective_id=0, has_side_effects=True, vmem_limit_bytes=64 * 2**20
        ),
        name="experts_backward",
    )(
        expert_ids.T,
        route_probs.T,
        grad_out,
        tokens,
        jnp.asarray(lmap),
        jnp.asarray(fold, BF16),
        jnp.asarray(unfold, BF16),
        w,
        w2,
        pre,
    )
    grad = dw[: 3 * hidden].reshape(3, hidden, width)
    return gt, jnp.transpose(grad, (2, 0, 1))[None]


def solution(mesh):
    in_specs = (
        P(("fsdp", "exp"), None),
        P(("fsdp", "exp"), None),
        P(("fsdp", "exp"), None),
        P(("fsdp", "exp"), None),
        P("exp", None, None, "fsdp"),
        P("exp", None, None, "fsdp"),
    )
    out_specs = (P(("fsdp", "exp"), None), P("exp", None, None, "fsdp"))
    return jax.shard_map(
        on_device, mesh=mesh, in_specs=in_specs, out_specs=out_specs, check_vma=False
    )
```

```python
import functools

import jax
import jax.numpy as jnp
import numpy as np
from jax import lax
from jax.experimental import pallas as pl
from jax.experimental.pallas import tpu as pltpu
from jax.sharding import PartitionSpec as P

MESH = pl.DeviceIdType.MESH
BF16 = jnp.bfloat16
F32 = jnp.float32
SIDE = 4
N_COPIES = 128


def round_up(value, unit):
    return -(-value // unit) * unit


def chunk_of(width):
    return 512 if width % 512 == 0 else 128


def dot(left, right, dims):
    return lax.dot_general(left, right, (dims, ((), ())), preferred_element_type=F32)


def rows_of(start, size):
    return pl.ds(pl.multiple_of(start, 16), size)


def cols_of(start, size):
    return pl.ds(pl.multiple_of(start, 128), size)


def kernel(
    cap,
    pieces,
    ids_ref,
    probs_ref,
    gout_ref,
    tok_ref,
    lmap_ref,
    fold_ref,
    unfold_ref,
    w_hbm,
    w3_hbm,
    pre_hbm,
    gt_ref,
    dw_hbm,
    g_buf,
    x_buf,
    w13,
    w2,
    pre,
    dgt,
    dg,
    sct,
    acc,
    stage,
    xmain,
    gmain,
    dxr,
    gext,
    gext_got,
    rext,
    rext_got,
    xext,
    xext_got,
    home,
    home_ext,
    send_sem,
    recv_sem,
    local_sem,
    credit_a,
    credit_b,
    credit_z,
):
    f = lax.axis_index("fsdp")
    e = lax.axis_index("exp")
    experts = lax.axis_size("exp")
    core = e % 2
    q = core * (f % SIDE) + (1 - core) * (f // SIDE)
    p = core * (f // SIDE) + (1 - core) * (f % SIDE)
    tokens, width = gout_ref.shape
    half = width // 2
    low, high = pl.ds(0, half), pl.ds(half, half)
    nc = chunk_of(width)
    steps = width // nc
    mb = cap // 16 * 16
    xb = cap - mb
    main = experts * mb
    rb = experts * cap
    rows = SIDE * rb
    rp = g_buf.shape[0]
    h2 = w13.shape[0] // SIDE
    h = h2 // 2
    hp = sct.shape[0] // SIDE
    piece = width // pieces

    def dev_at(pp, qq):
        return (SIDE * (core * pp + (1 - core) * qq) + core * qq + (1 - core) * pp, e)

    def dev_p(d):
        return dev_at((p + d) % SIDE, q)

    def dev_q(d):
        return dev_at(p, (q + d) % SIDE)

    def dev_e(d):
        return (f, (e + d) % experts)

    count = [0]

    def rcopy(src, dst, dev):
        i = count[0]
        count[0] += 1
        c = pltpu.make_async_remote_copy(
            src_ref=src,
            dst_ref=dst,
            send_sem=send_sem.at[i],
            recv_sem=recv_sem.at[i],
            device_id=dev,
            device_id_type=MESH,
        )
        c.start()
        return c

    def signal(sem, devs):
        for dev in devs:
            pl.semaphore_signal(sem, inc=1, device_id=dev, device_id_type=MESH)

    barrier = pltpu.get_barrier_semaphore()
    peers = [dev_p(d) for d in (1, 2, 3)] + [dev_q(d) for d in (1, 2, 3)]
    peers += [dev_e(d) for d in range(1, experts)]
    signal(barrier, peers)
    pl.semaphore_wait(barrier, len(peers))

    def view(ref, where, cols):
        return ref.at[where, :, cols] if len(ref.shape) == 3 else ref.at[where, cols]

    def ring_start(src, buf, off, pos, dev):
        mine = buf.at[off(pos)]
        return [rcopy(src, mine, dev(1)), rcopy(src, mine, dev(3))]

    def ring_forward(first, buf, off, pos, dev):
        first[0].wait_recv()
        part = view(buf, off((pos + 3) % SIDE), low)
        up = rcopy(part, part, dev(1))
        first[1].wait_recv()
        part = view(buf, off((pos + 1) % SIDE), high)
        down = rcopy(part, part, dev(3))
        return [up, down]

    def wait_recv(copies):
        for c in copies:
            c.wait_recv()

    def wait_send(copies):
        for c in copies:
            c.wait_send()

    w2_off = lambda j: j
    w13_off = lambda j: rows_of(h2 * j, h2)
    row_off = lambda b: rows_of(rb * b, rb)
    ext_off = lambda b: rows_of(rb * b + main, 16)
    w13_src = w_hbm.at[pl.ds(0, h2)]
    my_pre = pl.ds(pl.multiple_of(q * rp, 128), rp)

    w2_copies = ring_start(w3_hbm.at[2], w2, w2_off, q, dev_q)
    w13_copies = ring_start(w13_src, w13, w13_off, q, dev_q)
    strip = pre_hbm.shape[2] // 2
    local = [
        pltpu.make_async_copy(
            pre_hbm.at[i % 2, :, pl.ds(i // 2 * strip, strip)],
            stage.at[i, :, pl.ds(0, strip)],
            local_sem.at[i],
        )
        for i in range(4)
    ]
    local += [
        pltpu.make_async_copy(w3_hbm.at[2], w2.at[w2_off(q)], local_sem.at[4]),
        pltpu.make_async_copy(w13_src, w13.at[w13_off(q)], local_sem.at[5]),
    ]
    for c in local:
        c.start()

    ids = ids_ref[...]
    probs = probs_ref[...].astype(F32)
    kinds = lax.broadcasted_iota(jnp.int32, (experts, tokens), 0)
    hit = [(kinds == ids[k : k + 1, :]).astype(F32) for k in (0, 1)]
    earlier = (
        lax.broadcasted_iota(jnp.int32, (tokens, tokens), 0)
        < lax.broadcasted_iota(jnp.int32, (tokens, tokens), 1)
    ).astype(F32).astype(BF16)
    before = dot((hit[0] + hit[1]).astype(BF16), earlier, ((1,), (0,)))
    at_main, at_ext = [], []
    for k in (0, 1):
        own = ids[k : k + 1, :]
        slot = jnp.sum(before * hit[k], axis=0, keepdims=True).astype(jnp.int32)
        inside = slot < mb
        at_main.append(jnp.where(inside, mb * own + slot, -4096))
        at_ext.append(jnp.where(inside, -4096, 16 * own + pieces * (slot - mb)))

    def one_hot(size, where):
        line = lax.broadcasted_iota(jnp.int32, (size, tokens), 0)
        return [(line == w).astype(F32) for w in where]

    def dispatch(source, weights, big, small):
        pick = one_hot(main, at_main)
        if weights is None:
            home[...] = jnp.transpose(pick[0] + pick[1]).astype(BF16)
            pick = (pick[0] + pick[1]).astype(BF16)
        else:
            pick = (pick[0] * weights[0:1, :] + pick[1] * weights[1:2, :]).astype(BF16)

        def pick_step(n, _):
            cols = cols_of(n * nc, nc)
            big[:, cols] = dot(pick, source[:, cols], ((1,), (0,))).astype(BF16)
            return 0

        lax.fori_loop(0, steps, pick_step, 0)
        folded = jnp.zeros((experts * 16, piece), F32)
        for j in range(pieces):
            pick = one_hot(experts * 16, [w + j for w in at_ext])
            if weights is None:
                pick = pick[0] + pick[1]
                home_ext[pl.ds(j * tokens, tokens), :] = jnp.transpose(pick).astype(BF16)
            else:
                pick = pick[0] * weights[0:1, :] + pick[1] * weights[1:2, :]
            folded += dot(pick.astype(BF16), source[:, pl.ds(j * piece, piece)], ((1,), (0,)))
        small[...] = folded.astype(BF16)

    my_slots = rows_of(rb * p + mb * e, mb)

    def exchange(big, small, buf, small_got):
        copies = []
        for d in range(1, experts):
            to = (e + d) % experts
            there = p if d % 2 == 0 else q
            copies += [
                rcopy(
                    big.at[rows_of(mb * to, mb)],
                    buf.at[rows_of(rb * there + mb * e, mb)],
                    dev_e(d),
                ),
                rcopy(small.at[rows_of(16 * to, 16)], small_got.at[rows_of(16 * e, 16)], dev_e(d)),
            ]
        buf[my_slots, :] = big[rows_of(mb * e, mb), :]
        small_got[rows_of(16 * e, 16), :] = small[rows_of(16 * e, 16), :]
        return copies

    def unfold(buf, small_got):
        for j in range(pieces):
            buf[ext_off(p), pl.ds(j * piece, piece)] = dot(
                unfold_ref[pl.ds(16 * j, 16), :], small_got[...], ((1,), (0,))
            ).astype(BF16)

    dispatch(gout_ref, probs, gmain, gext)
    g_sent = exchange(gmain, gext, g_buf, gext_got)
    dispatch(tok_ref, None, xmain, xext)
    blank = pl.ds(rows, rp - rows)
    g_buf[blank, :] = jnp.zeros((rp - rows, width), BF16)
    x_buf[blank, :] = jnp.zeros((rp - rows, width), BF16)

    for c in local[:4]:
        c.wait()
    span = rp // 3
    line = lax.broadcasted_iota(jnp.int32, (span, span), 0)
    lane = lax.broadcasted_iota(jnp.int32, (span, span), 1)

    def regroup(to, _):
        for n in range(3):
            total = [jnp.zeros((h, span), F32)] * 2
            source = lmap_ref[0:1, pl.ds(n * span, span)]
            for b in (n, n + 1):
                block = core * (SIDE * b + to) + (1 - core) * (SIDE * to + b)
                start = rb * (block % 8)
                window = cols_of(start // 128 * 128, span)
                at = lane + (n * span - rb * b)
                match = (at >= 0) & (at < rb) & (line - start % 128 == source)
                match = match.astype(F32).astype(BF16)
                total = [
                    total[i] + dot(stage[block // 8 * 2 + i, :, window], match, ((1,), (0,)))
                    for i in (0, 1)
                ]
            both = jnp.concatenate(total, 0).astype(BF16)
            dgt[rows_of(h2 * to, h2), pl.ds(n * span, span)] = both
        return 0

    lax.fori_loop(0, SIDE, regroup, 0)
    pre_copies = [
        rcopy(dgt.at[rows_of(h2 * ((q + d) % SIDE), h2)], pre.at[:, my_pre], dev_q(d))
        for d in (1, 2, 3)
    ]
    own_pre = pltpu.make_async_copy(dgt.at[rows_of(h2 * q, h2)], pre.at[:, my_pre], local_sem.at[0])
    own_pre.start()

    w2_copies += ring_forward(w2_copies, w2, w2_off, q, dev_q)

    wait_recv(g_sent)
    unfold(g_buf, gext_got)
    g_copies = ring_start(g_buf.at[row_off(p)], g_buf, row_off, p, dev_p)

    x_sent = exchange(xmain, xext, x_buf, xext_got)
    w13_copies += ring_forward(w13_copies, w13, w13_off, q, dev_q)
    g_copies += ring_forward(g_copies, g_buf, row_off, p, dev_p)
    wait_recv(x_sent)
    unfold(x_buf, xext_got)
    x_copies = ring_start(x_buf.at[row_off(p)], x_buf, row_off, p, dev_p)

    wait_send(g_sent)
    signal(credit_z, [dev_e(d) for d in range(1, experts)])
    local[4].wait()
    local[5].wait()
    wait_recv(w2_copies[2:])
    wait_recv(g_copies[2:])

    acc[...] = jnp.zeros_like(acc)

    def back_step(n, _):
        cols = cols_of(n * nc, nc)
        rows_g = g_buf[:, cols]
        for j in range(SIDE):
            acc[pl.ds(h * j, h), :] += dot(w2[j, :, cols], rows_g, ((1,), (1,)))
        return 0

    lax.fori_loop(0, steps, back_step, 0)
    wait_recv(pre_copies)
    wait_send(pre_copies)
    own_pre.wait()

    def activate(i, _):
        j, c = i // (rp // 128), i % (rp // 128)
        lanes = cols_of(c * 128, 128)
        saved = pre[:, cols_of(j * rp + c * 128, 128)].astype(F32)
        back = acc[pl.ds(pl.multiple_of(h * j, 8), h), lanes]
        a, b = saved[:h], saved[h:]
        sig = jax.nn.sigmoid(a)
        act = a * sig
        d_gate = back * b * sig * (1.0 + a * (1.0 - sig))
        d_up = back * act
        dgt[rows_of(h2 * j, h2), lanes] = jnp.concatenate([d_gate, d_up], 0).astype(BF16)
        scaled = jnp.concatenate([act * b, jnp.zeros((hp - h, 128), F32)], 0)
        sct[rows_of(hp * j, hp), lanes] = scaled.astype(BF16)
        return 0

    lax.fori_loop(0, SIDE * (rp // 128), activate, 0)

    wait_send(w2_copies)
    signal(credit_a, [dev_q(1), dev_q(3)])

    def send_far(part, off, pos, dst, dev):
        far = off((pos + 2) % SIDE)
        return [
            rcopy(view(part, far, low), dst.at[:, low], dev(1)),
            rcopy(view(part, far, high), dst.at[:, high], dev(3)),
        ]

    def send_near_direct(part, off, pos, dst, dev):
        return [
            rcopy(view(part, off((pos + 1) % SIDE), high), dst[0].at[:, high], dev(1)),
            rcopy(view(part, off((pos + 3) % SIDE), low), dst[1].at[:, low], dev(3)),
        ]

    def add_into(part, where, others, start, size, out=None):
        ac = 256 if half % 256 == 0 else 128

        def add_step(n, _):
            cols = cols_of(start + n * ac, ac)
            mine = view(part, where, cols)
            total = mine[...].astype(F32)
            for ref in others:
                total = total + ref[:, cols].astype(F32)
            if out is None:
                mine[...] = total.astype(BF16)
            else:
                for i in (0, 1):
                    out[i][:, cols] = total[h * i : h * (i + 1)].astype(BF16)
            return 0

        lax.fori_loop(0, size // ac, add_step, 0)

    def send_near_added(far, part, off, pos, got, dst, dev):
        far[0].wait_recv()
        where = off((pos + 1) % SIDE)
        add_into(part, where, [got], 0, half)
        up = rcopy(view(part, where, low), dst[0].at[:, low], dev(1))
        far[1].wait_recv()
        where = off((pos + 3) % SIDE)
        add_into(part, where, [got], half, half)
        down = rcopy(view(part, where, high), dst[1].at[:, high], dev(3))
        return [up, down]

    wait_send(x_sent)

    def dw2_step(n, _):
        cols = cols_of(n * nc, nc)
        part = dot(sct[...], g_buf[:, cols], ((1,), (0,)))
        for j in range(SIDE):
            stage[j, :, cols] = part[hp * j : hp * j + h].astype(BF16)
        return 0

    lax.fori_loop(0, steps, dw2_step, 0)
    pl.semaphore_wait(credit_a, 2)
    dw2_near = [w2.at[1], w2.at[2]]
    dw2_far_got = w2.at[0]
    dw2_far = send_far(stage, w2_off, q, dw2_far_got, dev_q)
    x_copies += ring_forward(x_copies, x_buf, row_off, p, dev_p)

    def flip(c, _):
        lanes = cols_of(c * 128, 128)
        dg[rows_of(c * 128, 128), :] = jnp.transpose(dgt[:, lanes])
        return 0

    lax.fori_loop(0, rp // 128, flip, 0)

    wait_send(g_copies)
    wait_recv(w13_copies[2:])

    def dx_block(d):
        b = (p + d) % SIDE

        def dx_step(n, _):
            cols = cols_of(n * nc, nc)
            g_buf[row_off(b), cols] = dot(dg[row_off(b), :], w13[:, cols], ((1,), (0,))).astype(BF16)
            return 0

        lax.fori_loop(0, steps, dx_step, 0)

    dx_far_got = dxr.at[pl.ds(0, rb), pl.ds(0, width)]
    dx_near = [dxr.at[pl.ds(rb * i, rb), pl.ds(0, width)] for i in (1, 2)]
    dx_block(2)
    dx_far = send_far(g_buf, row_off, p, dx_far_got, dev_p)
    dx_block(1)
    dx_block(3)
    dx_mid = send_near_direct(g_buf, row_off, p, dx_near, dev_p)
    dx_block(0)
    dx_mid += send_near_added(dx_far, g_buf, row_off, p, dx_far_got, dx_near, dev_p)
    dw2_mid = send_near_direct(stage, w2_off, q, dw2_near, dev_q)
    dw2_mid += send_near_added(dw2_far, stage, w2_off, q, dw2_far_got, dw2_near, dev_q)

    wait_recv(x_copies[2:])
    wait_send(w13_copies)

    def dw13_block(d):
        j = (q + d) % SIDE

        def dw13_step(n, _):
            cols = cols_of(n * nc, nc)
            w13[w13_off(j), cols] = dot(
                dgt[w13_off(j), :], x_buf[:, cols], ((1,), (0,))
            ).astype(BF16)
            return 0

        lax.fori_loop(0, steps, dw13_step, 0)

    dw13_far_got = pre.at[:, pl.ds(0, width)]
    dw13_near = [x_buf.at[pl.ds(0, h2)], x_buf.at[pl.ds(h2, h2)]]
    dw13_block(2)
    dw13_far = send_far(w13, w13_off, q, dw13_far_got, dev_q)
    dw13_block(1)
    dw13_block(3)
    dw13_block(0)
    wait_send(x_copies)
    signal(credit_b, [dev_q(1), dev_q(3)])
    pl.semaphore_wait(credit_b, 2)
    dw13_mid = send_near_direct(w13, w13_off, q, dw13_near, dev_q)
    wait_recv(dx_mid)
    add_into(g_buf, row_off(p), dx_near, 0, width)
    folded = jnp.zeros((experts * 16, piece), F32)
    for j in range(pieces):
        folded += dot(
            fold_ref[pl.ds(j * experts * 16, experts * 16), :],
            g_buf[ext_off(p), pl.ds(j * piece, piece)],
            ((1,), (0,)),
        )
    rext[...] = folded.astype(BF16)
    pl.semaphore_wait(credit_z, experts - 1)
    ret = []
    for d in range(1, experts):
        to = (e + d) % experts
        ret.append(
            rcopy(
                g_buf.at[rows_of(rb * p + mb * to, mb)], gmain.at[rows_of(mb * e, mb)], dev_e(d)
            )
        )
        ret.append(
            rcopy(rext.at[rows_of(16 * to, 16)], rext_got.at[rows_of(16 * e, 16)], dev_e(d))
        )
    gmain[rows_of(mb * e, mb), :] = g_buf[my_slots, :]
    rext_got[rows_of(16 * e, 16), :] = rext[rows_of(16 * e, 16), :]

    dw13_mid += send_near_added(dw13_far, w13, w13_off, q, dw13_far_got, dw13_near, dev_q)

    wait_recv(dw2_mid)
    add_into(stage, w2_off(q), dw2_near, 0, width)
    full = pl.ds(0, width)
    outs = [pltpu.make_async_copy(stage.at[q, :, full], dw_hbm.at[2], local_sem.at[2])]
    outs[0].start()

    wait_recv(ret)
    for j in range(pieces):
        cols = pl.ds(j * piece, piece)
        total = dot(home[...], gmain[:, cols], ((1,), (0,)))
        total += dot(home_ext[pl.ds(j * tokens, tokens), :], rext_got[...], ((1,), (0,)))
        gt_ref[:, cols] = total.astype(BF16)

    wait_send(dw2_far + dw2_mid)
    wait_recv(dw13_mid)
    sums = [stage.at[(q + 1 + i) % SIDE] for i in (0, 1)]
    add_into(w13, w13_off(q), dw13_near, 0, width, sums)
    for i in (0, 1):
        outs.append(pltpu.make_async_copy(sums[i].at[:, full], dw_hbm.at[i], local_sem.at[i]))
        outs[-1].start()

    wait_send(dx_far + dx_mid + dw13_far + dw13_mid + ret)
    for c in outs:
        c.wait()


def on_device(tokens, grad_out, route_probs, expert_ids, saved_pre, expert_weights):
    rows, width = tokens.shape
    experts = lax.axis_size("exp")
    cap = 17 * rows // (8 * experts)
    mb = cap // 16 * 16
    xb = cap - mb
    main = experts * mb
    rb = experts * cap
    hidden = expert_weights.shape[3]
    hp = round_up(hidden, 16)
    rp = round_up(SIDE * rb + 64, 128)
    strip = saved_pre.shape[1] // 2
    pieces = max(k for k in range(1, 16 // xb + 1) if width % (128 * k) == 0)
    w3 = jnp.transpose(expert_weights[0], (1, 2, 0))
    pre = jnp.transpose(saved_pre[0], (1, 2, 0))

    at = np.arange(rb)
    in_main = at // mb * cap + at % mb
    in_ext = (at - main) // xb * cap + mb + (at - main) % xb
    lmap = np.full((8, rp), -1, np.int32)
    lmap[:, : SIDE * rb] = np.tile(np.where(at < main, in_main, in_ext), SIDE)
    ext = np.arange(16)
    unfold = np.zeros((pieces, 16, experts * 16), np.float32)
    for j in range(pieces):
        unfold[j, ext, 16 * (ext // xb) + pieces * (ext % xb) + j] = 1
    fold = unfold.transpose(0, 2, 1).reshape(pieces * experts * 16, 16)
    unfold = unfold.reshape(pieces * 16, experts * 16)

    vmem = pl.BlockSpec(memory_space=pltpu.VMEM)
    hbm = pl.BlockSpec(memory_space=pl.ANY)
    gt, dw = pl.pallas_call(
        functools.partial(kernel, cap, pieces),
        out_shape=(
            jax.ShapeDtypeStruct((rows, width), BF16),
            jax.ShapeDtypeStruct((3, hidden, width), BF16),
        ),
        in_specs=[vmem] * 7 + [hbm] * 3,
        out_specs=(vmem, hbm),
        scratch_shapes=[
            pltpu.VMEM((rp, width), BF16),
            pltpu.VMEM((rp, width), BF16),
            pltpu.VMEM((SIDE * 2 * hidden, width), BF16),
            pltpu.VMEM((SIDE, hidden, width), BF16),
            pltpu.VMEM((2 * hidden, SIDE * rp), BF16),
            pltpu.VMEM((SIDE * 2 * hidden, rp), BF16),
            pltpu.VMEM((rp, SIDE * 2 * hidden), BF16),
            pltpu.VMEM((SIDE * hp, rp), BF16),
            pltpu.VMEM((SIDE * hidden, rp), F32),
            pltpu.VMEM((SIDE, hidden, max(width, strip)), BF16),
            pltpu.VMEM((main, width), BF16),
            pltpu.VMEM((main, width), BF16),
            pltpu.VMEM((3 * rb, width), BF16),
            pltpu.VMEM((experts * 16, width // pieces), BF16),
            pltpu.VMEM((experts * 16, width // pieces), BF16),
            pltpu.VMEM((experts * 16, width // pieces), BF16),
            pltpu.VMEM((experts * 16, width // pieces), BF16),
            pltpu.VMEM((experts * 16, width // pieces), BF16),
            pltpu.VMEM((experts * 16, width // pieces), BF16),
            pltpu.VMEM((rows, main), BF16),
            pltpu.VMEM((pieces * rows, experts * 16), BF16),
            pltpu.SemaphoreType.DMA((N_COPIES,)),
            pltpu.SemaphoreType.DMA((N_COPIES,)),
            pltpu.SemaphoreType.DMA((6,)),
            pltpu.SemaphoreType.REGULAR,
            pltpu.SemaphoreType.REGULAR,
            pltpu.SemaphoreType.REGULAR,
        ],
        compiler_params=pltpu.CompilerParams(
            collective_id=0, has_side_effects=True, vmem_limit_bytes=64 * 2**20
        ),
        name="experts_backward",
    )(
        expert_ids.T,
        route_probs.T,
        grad_out,
        tokens,
        jnp.asarray(lmap),
        jnp.asarray(fold, BF16),
        jnp.asarray(unfold, BF16),
        w3.reshape(3 * hidden, width),
        w3,
        pre,
    )
    return gt, jnp.transpose(dw, (2, 0, 1))[None]


def solution(mesh):
    in_specs = (
        P(("fsdp", "exp"), None),
        P(("fsdp", "exp"), None),
        P(("fsdp", "exp"), None),
        P(("fsdp", "exp"), None),
        P("exp", None, None, "fsdp"),
        P("exp", None, None, "fsdp"),
    )
    out_specs = (P(("fsdp", "exp"), None), P("exp", None, None, "fsdp"))
    return jax.shard_map(
        on_device, mesh=mesh, in_specs=in_specs, out_specs=out_specs, check_vma=False
    )
```

```python
import functools

import jax
import jax.numpy as jnp
import numpy as np
from jax import lax
from jax.experimental import pallas as pl
from jax.experimental.pallas import tpu as pltpu
from jax.sharding import PartitionSpec as P

MESH = pl.DeviceIdType.MESH
BF16 = jnp.bfloat16
F32 = jnp.float32
SIDE = 4
N_COPIES = 128


def round_up(value, unit):
    return -(-value // unit) * unit


def chunk_of(width):
    return 512 if width % 512 == 0 else 128


def dot(left, right, dims):
    return lax.dot_general(left, right, (dims, ((), ())), preferred_element_type=F32)


def rows_of(start, size):
    return pl.ds(pl.multiple_of(start, 16), size)


def cols_of(start, size):
    return pl.ds(pl.multiple_of(start, 128), size)


def kernel(
    cap,
    pieces,
    ids_ref,
    probs_ref,
    gout_ref,
    tok_ref,
    lmap_ref,
    fold_ref,
    unfold_ref,
    w_hbm,
    w3_hbm,
    pre_hbm,
    gt_ref,
    dw_hbm,
    g_buf,
    x_buf,
    w13,
    w2,
    pre,
    dgt,
    dg,
    sct,
    acc,
    stage,
    xmain,
    gmain,
    dxr,
    gext,
    gext_got,
    rext,
    rext_got,
    xext,
    xext_got,
    home,
    home_ext,
    send_sem,
    recv_sem,
    local_sem,
    credit_a,
    credit_b,
    credit_z,
):
    f = lax.axis_index("fsdp")
    e = lax.axis_index("exp")
    experts = lax.axis_size("exp")
    core = e % 2
    q = core * (f % SIDE) + (1 - core) * (f // SIDE)
    p = core * (f // SIDE) + (1 - core) * (f % SIDE)
    tokens, width = gout_ref.shape
    half = width // 2
    low, high = pl.ds(0, half), pl.ds(half, half)
    nc = chunk_of(width)
    steps = width // nc
    mb = cap // 16 * 16
    xb = cap - mb
    main = experts * mb
    rb = experts * cap
    rows = SIDE * rb
    rp = g_buf.shape[0]
    h2 = w13.shape[0] // SIDE
    h = h2 // 2
    hp = sct.shape[0] // SIDE
    piece = width // pieces

    def dev_at(pp, qq):
        return (SIDE * (core * pp + (1 - core) * qq) + core * qq + (1 - core) * pp, e)

    def dev_p(d):
        return dev_at((p + d) % SIDE, q)

    def dev_q(d):
        return dev_at(p, (q + d) % SIDE)

    def dev_e(d):
        return (f, (e + d) % experts)

    count = [0]

    def rcopy(src, dst, dev):
        i = count[0]
        count[0] += 1
        c = pltpu.make_async_remote_copy(
            src_ref=src,
            dst_ref=dst,
            send_sem=send_sem.at[i],
            recv_sem=recv_sem.at[i],
            device_id=dev,
            device_id_type=MESH,
        )
        c.start()
        return c

    def signal(sem, devs):
        for dev in devs:
            pl.semaphore_signal(sem, inc=1, device_id=dev, device_id_type=MESH)

    barrier = pltpu.get_barrier_semaphore()
    peers = [dev_p(d) for d in (1, 2, 3)] + [dev_q(d) for d in (1, 2, 3)]
    peers += [dev_e(d) for d in range(1, experts)]
    signal(barrier, peers)
    pl.semaphore_wait(barrier, len(peers))

    def view(ref, where, cols):
        return ref.at[where, :, cols] if len(ref.shape) == 3 else ref.at[where, cols]

    def ring_start(src, buf, off, pos, dev):
        return [
            rcopy(src.at[:, cols], view(buf, off(pos), cols), dev(d))
            for d, cols in ((1, low), (3, high), (1, high), (3, low))
        ]

    def ring_forward(first, buf, off, pos, dev):
        first[0].wait_recv()
        part = view(buf, off((pos + 3) % SIDE), low)
        up = rcopy(part, part, dev(1))
        first[1].wait_recv()
        part = view(buf, off((pos + 1) % SIDE), high)
        down = rcopy(part, part, dev(3))
        return [up, down]

    def wait_recv(copies):
        for c in copies:
            c.wait_recv()

    def wait_send(copies):
        for c in copies:
            c.wait_send()

    w2_off = lambda j: j
    w13_off = lambda j: rows_of(h2 * j, h2)
    row_off = lambda b: rows_of(rb * b, rb)
    ext_off = lambda b: rows_of(rb * b + main, 16)
    w13_src = w_hbm.at[pl.ds(0, h2)]
    my_pre = pl.ds(pl.multiple_of(q * rp, 128), rp)

    w2_copies = ring_start(w3_hbm.at[2], w2, w2_off, q, dev_q)
    w13_copies = ring_start(w13_src, w13, w13_off, q, dev_q)
    strip = pre_hbm.shape[2] // 2
    local = [
        pltpu.make_async_copy(
            pre_hbm.at[i % 2, :, pl.ds(i // 2 * strip, strip)],
            stage.at[i, :, pl.ds(0, strip)],
            local_sem.at[i],
        )
        for i in range(4)
    ]
    local += [
        pltpu.make_async_copy(w3_hbm.at[2], w2.at[w2_off(q)], local_sem.at[4]),
        pltpu.make_async_copy(w13_src, w13.at[w13_off(q)], local_sem.at[5]),
    ]
    for c in local:
        c.start()

    ids = ids_ref[...]
    probs = probs_ref[...].astype(F32)
    kinds = lax.broadcasted_iota(jnp.int32, (experts, tokens), 0)
    hit = [(kinds == ids[k : k + 1, :]).astype(F32) for k in (0, 1)]
    earlier = (
        lax.broadcasted_iota(jnp.int32, (tokens, tokens), 0)
        < lax.broadcasted_iota(jnp.int32, (tokens, tokens), 1)
    ).astype(F32).astype(BF16)
    before = dot((hit[0] + hit[1]).astype(BF16), earlier, ((1,), (0,)))
    at_main, at_ext = [], []
    for k in (0, 1):
        own = ids[k : k + 1, :]
        slot = jnp.sum(before * hit[k], axis=0, keepdims=True).astype(jnp.int32)
        inside = slot < mb
        at_main.append(jnp.where(inside, mb * own + slot, -4096))
        at_ext.append(jnp.where(inside, -4096, 16 * own + pieces * (slot - mb)))

    def one_hot(size, where):
        line = lax.broadcasted_iota(jnp.int32, (size, tokens), 0)
        return [(line == w).astype(F32) for w in where]

    def dispatch(source, weights, big, small):
        pick = one_hot(main, at_main)
        if weights is None:
            home[...] = jnp.transpose(pick[0] + pick[1]).astype(BF16)
            pick = (pick[0] + pick[1]).astype(BF16)
        else:
            pick = (pick[0] * weights[0:1, :] + pick[1] * weights[1:2, :]).astype(BF16)

        def pick_step(n, _):
            cols = cols_of(n * nc, nc)
            big[:, cols] = dot(pick, source[:, cols], ((1,), (0,))).astype(BF16)
            return 0

        lax.fori_loop(0, steps, pick_step, 0)
        folded = jnp.zeros((experts * 16, piece), F32)
        for j in range(pieces):
            pick = one_hot(experts * 16, [w + j for w in at_ext])
            if weights is None:
                pick = pick[0] + pick[1]
                home_ext[pl.ds(j * tokens, tokens), :] = jnp.transpose(pick).astype(BF16)
            else:
                pick = pick[0] * weights[0:1, :] + pick[1] * weights[1:2, :]
            folded += dot(pick.astype(BF16), source[:, pl.ds(j * piece, piece)], ((1,), (0,)))
        small[...] = folded.astype(BF16)

    my_slots = rows_of(rb * p + mb * e, mb)

    def exchange(big, small, buf, small_got):
        copies = []
        for d in range(1, experts):
            to = (e + d) % experts
            there = p if d % 2 == 0 else q
            copies += [
                rcopy(
                    big.at[rows_of(mb * to, mb)],
                    buf.at[rows_of(rb * there + mb * e, mb)],
                    dev_e(d),
                ),
                rcopy(small.at[rows_of(16 * to, 16)], small_got.at[rows_of(16 * e, 16)], dev_e(d)),
            ]
        buf[my_slots, :] = big[rows_of(mb * e, mb), :]
        small_got[rows_of(16 * e, 16), :] = small[rows_of(16 * e, 16), :]
        return copies

    def unfold(buf, small_got):
        for j in range(pieces):
            buf[ext_off(p), pl.ds(j * piece, piece)] = dot(
                unfold_ref[pl.ds(16 * j, 16), :], small_got[...], ((1,), (0,))
            ).astype(BF16)

    dispatch(gout_ref, probs, gmain, gext)
    g_sent = exchange(gmain, gext, g_buf, gext_got)
    dispatch(tok_ref, None, xmain, xext)
    blank = pl.ds(rows, rp - rows)
    g_buf[blank, :] = jnp.zeros((rp - rows, width), BF16)
    x_buf[blank, :] = jnp.zeros((rp - rows, width), BF16)

    for c in local[:4]:
        c.wait()
    span = rp // 3
    line = lax.broadcasted_iota(jnp.int32, (span, span), 0)
    lane = lax.broadcasted_iota(jnp.int32, (span, span), 1)

    def regroup(to, _):
        for n in range(3):
            total = [jnp.zeros((h, span), F32)] * 2
            source = lmap_ref[0:1, pl.ds(n * span, span)]
            for b in (n, n + 1):
                block = core * (SIDE * b + to) + (1 - core) * (SIDE * to + b)
                start = rb * (block % 8)
                window = cols_of(start // 128 * 128, span)
                at = lane + (n * span - rb * b)
                match = (at >= 0) & (at < rb) & (line - start % 128 == source)
                match = match.astype(F32).astype(BF16)
                total = [
                    total[i] + dot(stage[block // 8 * 2 + i, :, window], match, ((1,), (0,)))
                    for i in (0, 1)
                ]
            both = jnp.concatenate(total, 0).astype(BF16)
            dgt[rows_of(h2 * to, h2), pl.ds(n * span, span)] = both
        return 0

    lax.fori_loop(0, SIDE, regroup, 0)
    pre_copies = [
        rcopy(dgt.at[rows_of(h2 * ((q + d) % SIDE), h2)], pre.at[:, my_pre], dev_q(d))
        for d in (1, 2, 3)
    ]
    own_pre = pltpu.make_async_copy(dgt.at[rows_of(h2 * q, h2)], pre.at[:, my_pre], local_sem.at[0])
    own_pre.start()

    w2_copies += ring_forward(w2_copies, w2, w2_off, q, dev_q)

    wait_recv(g_sent)
    unfold(g_buf, gext_got)
    g_copies = ring_start(g_buf.at[row_off(p)], g_buf, row_off, p, dev_p)

    x_sent = exchange(xmain, xext, x_buf, xext_got)
    w13_copies += ring_forward(w13_copies, w13, w13_off, q, dev_q)
    g_copies += ring_forward(g_copies, g_buf, row_off, p, dev_p)
    wait_recv(x_sent)
    unfold(x_buf, xext_got)
    x_copies = ring_start(x_buf.at[row_off(p)], x_buf, row_off, p, dev_p)

    wait_send(g_sent)
    signal(credit_z, [dev_e(d) for d in range(1, experts)])
    local[4].wait()
    local[5].wait()
    wait_recv(w2_copies[2:])
    wait_recv(g_copies[2:])

    acc[...] = jnp.zeros_like(acc)

    def back_step(n, _):
        cols = cols_of(n * nc, nc)
        rows_g = g_buf[:, cols]
        for j in range(SIDE):
            acc[pl.ds(h * j, h), :] += dot(w2[j, :, cols], rows_g, ((1,), (1,)))
        return 0

    lax.fori_loop(0, steps, back_step, 0)
    wait_recv(pre_copies)
    wait_send(pre_copies)
    own_pre.wait()

    def activate(i, _):
        j, c = i // (rp // 128), i % (rp // 128)
        lanes = cols_of(c * 128, 128)
        saved = pre[:, cols_of(j * rp + c * 128, 128)].astype(F32)
        back = acc[pl.ds(pl.multiple_of(h * j, 8), h), lanes]
        a, b = saved[:h], saved[h:]
        sig = jax.nn.sigmoid(a)
        act = a * sig
        d_gate = back * b * sig * (1.0 + a * (1.0 - sig))
        d_up = back * act
        dgt[rows_of(h2 * j, h2), lanes] = jnp.concatenate([d_gate, d_up], 0).astype(BF16)
        scaled = jnp.concatenate([act * b, jnp.zeros((hp - h, 128), F32)], 0)
        sct[rows_of(hp * j, hp), lanes] = scaled.astype(BF16)
        return 0

    lax.fori_loop(0, SIDE * (rp // 128), activate, 0)

    wait_send(w2_copies)
    signal(credit_a, [dev_q(1), dev_q(3)])

    def send_far(part, off, pos, dst, dev):
        far = off((pos + 2) % SIDE)
        return [
            rcopy(view(part, far, low), dst.at[:, low], dev(1)),
            rcopy(view(part, far, high), dst.at[:, high], dev(3)),
        ]

    def send_near_direct(part, off, pos, dst, dev):
        return [
            rcopy(view(part, off((pos + 1) % SIDE), high), dst[0].at[:, high], dev(1)),
            rcopy(view(part, off((pos + 3) % SIDE), low), dst[1].at[:, low], dev(3)),
        ]

    def add_into(part, where, others, start, size, out=None):
        ac = 256 if half % 256 == 0 else 128

        def add_step(n, _):
            cols = cols_of(start + n * ac, ac)
            mine = view(part, where, cols)
            total = mine[...].astype(F32)
            for ref in others:
                total = total + ref[:, cols].astype(F32)
            if out is None:
                mine[...] = total.astype(BF16)
            else:
                for i in (0, 1):
                    out[i][:, cols] = total[h * i : h * (i + 1)].astype(BF16)
            return 0

        lax.fori_loop(0, size // ac, add_step, 0)

    def send_near_added(far, part, off, pos, got, dst, dev):
        far[0].wait_recv()
        where = off((pos + 1) % SIDE)
        add_into(part, where, [got], 0, half)
        up = rcopy(view(part, where, low), dst[0].at[:, low], dev(1))
        far[1].wait_recv()
        where = off((pos + 3) % SIDE)
        add_into(part, where, [got], half, half)
        down = rcopy(view(part, where, high), dst[1].at[:, high], dev(3))
        return [up, down]

    wait_send(x_sent)

    def dw2_step(n, _):
        cols = cols_of(n * nc, nc)
        part = dot(sct[...], g_buf[:, cols], ((1,), (0,)))
        for j in range(SIDE):
            stage[j, :, cols] = part[hp * j : hp * j + h].astype(BF16)
        return 0

    lax.fori_loop(0, steps, dw2_step, 0)
    pl.semaphore_wait(credit_a, 2)
    dw2_near = [w2.at[1], w2.at[2]]
    dw2_far_got = w2.at[0]
    dw2_far = send_far(stage, w2_off, q, dw2_far_got, dev_q)
    x_copies += ring_forward(x_copies, x_buf, row_off, p, dev_p)

    def flip(c, _):
        lanes = cols_of(c * 128, 128)
        dg[rows_of(c * 128, 128), :] = jnp.transpose(dgt[:, lanes])
        return 0

    lax.fori_loop(0, rp // 128, flip, 0)

    wait_send(g_copies)
    wait_recv(w13_copies[2:])

    def dx_block(d):
        b = (p + d) % SIDE

        def dx_step(n, _):
            cols = cols_of(n * nc, nc)
            g_buf[row_off(b), cols] = dot(dg[row_off(b), :], w13[:, cols], ((1,), (0,))).astype(BF16)
            return 0

        lax.fori_loop(0, steps, dx_step, 0)

    dx_far_got = dxr.at[pl.ds(0, rb), pl.ds(0, width)]
    dx_near = [dxr.at[pl.ds(rb * i, rb), pl.ds(0, width)] for i in (1, 2)]
    dx_block(2)
    dx_far = send_far(g_buf, row_off, p, dx_far_got, dev_p)
    dx_block(1)
    dx_block(3)
    dx_mid = send_near_direct(g_buf, row_off, p, dx_near, dev_p)
    dx_block(0)
    dx_mid += send_near_added(dx_far, g_buf, row_off, p, dx_far_got, dx_near, dev_p)
    dw2_mid = send_near_direct(stage, w2_off, q, dw2_near, dev_q)
    dw2_mid += send_near_added(dw2_far, stage, w2_off, q, dw2_far_got, dw2_near, dev_q)

    wait_recv(x_copies[2:])
    wait_send(w13_copies)

    def dw13_block(d):
        j = (q + d) % SIDE

        def dw13_step(n, _):
            cols = cols_of(n * nc, nc)
            w13[w13_off(j), cols] = dot(
                dgt[w13_off(j), :], x_buf[:, cols], ((1,), (0,))
            ).astype(BF16)
            return 0

        lax.fori_loop(0, steps, dw13_step, 0)

    dw13_far_got = pre.at[:, pl.ds(0, width)]
    dw13_near = [x_buf.at[pl.ds(0, h2)], x_buf.at[pl.ds(h2, h2)]]
    dw13_block(2)
    dw13_far = send_far(w13, w13_off, q, dw13_far_got, dev_q)
    dw13_block(1)
    dw13_block(3)
    dw13_block(0)
    wait_send(x_copies)
    signal(credit_b, [dev_q(1), dev_q(3)])
    pl.semaphore_wait(credit_b, 2)
    dw13_mid = send_near_direct(w13, w13_off, q, dw13_near, dev_q)
    wait_recv(dx_mid)
    add_into(g_buf, row_off(p), dx_near, 0, width)
    folded = jnp.zeros((experts * 16, piece), F32)
    for j in range(pieces):
        folded += dot(
            fold_ref[pl.ds(j * experts * 16, experts * 16), :],
            g_buf[ext_off(p), pl.ds(j * piece, piece)],
            ((1,), (0,)),
        )
    rext[...] = folded.astype(BF16)
    pl.semaphore_wait(credit_z, experts - 1)
    ret = []
    for d in range(1, experts):
        to = (e + d) % experts
        ret.append(
            rcopy(
                g_buf.at[rows_of(rb * p + mb * to, mb)], gmain.at[rows_of(mb * e, mb)], dev_e(d)
            )
        )
        ret.append(
            rcopy(rext.at[rows_of(16 * to, 16)], rext_got.at[rows_of(16 * e, 16)], dev_e(d))
        )
    gmain[rows_of(mb * e, mb), :] = g_buf[my_slots, :]
    rext_got[rows_of(16 * e, 16), :] = rext[rows_of(16 * e, 16), :]

    dw13_mid += send_near_added(dw13_far, w13, w13_off, q, dw13_far_got, dw13_near, dev_q)

    wait_recv(dw2_mid)
    add_into(stage, w2_off(q), dw2_near, 0, width)
    full = pl.ds(0, width)
    outs = [pltpu.make_async_copy(stage.at[q, :, full], dw_hbm.at[2], local_sem.at[2])]
    outs[0].start()

    wait_recv(ret)
    for j in range(pieces):
        cols = pl.ds(j * piece, piece)
        total = dot(home[...], gmain[:, cols], ((1,), (0,)))
        total += dot(home_ext[pl.ds(j * tokens, tokens), :], rext_got[...], ((1,), (0,)))
        gt_ref[:, cols] = total.astype(BF16)

    wait_send(dw2_far + dw2_mid)
    wait_recv(dw13_mid)
    sums = [stage.at[(q + 1 + i) % SIDE] for i in (0, 1)]
    add_into(w13, w13_off(q), dw13_near, 0, width, sums)
    for i in (0, 1):
        outs.append(pltpu.make_async_copy(sums[i].at[:, full], dw_hbm.at[i], local_sem.at[i]))
        outs[-1].start()

    wait_send(dx_far + dx_mid + dw13_far + dw13_mid + ret)
    for c in outs:
        c.wait()


def on_device(tokens, grad_out, route_probs, expert_ids, saved_pre, expert_weights):
    rows, width = tokens.shape
    experts = lax.axis_size("exp")
    cap = 17 * rows // (8 * experts)
    mb = cap // 16 * 16
    xb = cap - mb
    main = experts * mb
    rb = experts * cap
    hidden = expert_weights.shape[3]
    hp = round_up(hidden, 16)
    rp = round_up(SIDE * rb + 64, 128)
    strip = saved_pre.shape[1] // 2
    pieces = max(k for k in range(1, 16 // xb + 1) if width % (128 * k) == 0)
    w3 = jnp.transpose(expert_weights[0], (1, 2, 0))
    pre = jnp.transpose(saved_pre[0], (1, 2, 0))

    at = np.arange(rb)
    in_main = at // mb * cap + at % mb
    in_ext = (at - main) // xb * cap + mb + (at - main) % xb
    lmap = np.full((8, rp), -1, np.int32)
    lmap[:, : SIDE * rb] = np.tile(np.where(at < main, in_main, in_ext), SIDE)
    ext = np.arange(16)
    unfold = np.zeros((pieces, 16, experts * 16), np.float32)
    for j in range(pieces):
        unfold[j, ext, 16 * (ext // xb) + pieces * (ext % xb) + j] = 1
    fold = unfold.transpose(0, 2, 1).reshape(pieces * experts * 16, 16)
    unfold = unfold.reshape(pieces * 16, experts * 16)

    vmem = pl.BlockSpec(memory_space=pltpu.VMEM)
    hbm = pl.BlockSpec(memory_space=pl.ANY)
    gt, dw = pl.pallas_call(
        functools.partial(kernel, cap, pieces),
        out_shape=(
            jax.ShapeDtypeStruct((rows, width), BF16),
            jax.ShapeDtypeStruct((3, hidden, width), BF16),
        ),
        in_specs=[vmem] * 7 + [hbm] * 3,
        out_specs=(vmem, hbm),
        scratch_shapes=[
            pltpu.VMEM((rp, width), BF16),
            pltpu.VMEM((rp, width), BF16),
            pltpu.VMEM((SIDE * 2 * hidden, width), BF16),
            pltpu.VMEM((SIDE, hidden, width), BF16),
            pltpu.VMEM((2 * hidden, SIDE * rp), BF16),
            pltpu.VMEM((SIDE * 2 * hidden, rp), BF16),
            pltpu.VMEM((rp, SIDE * 2 * hidden), BF16),
            pltpu.VMEM((SIDE * hp, rp), BF16),
            pltpu.VMEM((SIDE * hidden, rp), F32),
            pltpu.VMEM((SIDE, hidden, max(width, strip)), BF16),
            pltpu.VMEM((main, width), BF16),
            pltpu.VMEM((main, width), BF16),
            pltpu.VMEM((3 * rb, width), BF16),
            pltpu.VMEM((experts * 16, width // pieces), BF16),
            pltpu.VMEM((experts * 16, width // pieces), BF16),
            pltpu.VMEM((experts * 16, width // pieces), BF16),
            pltpu.VMEM((experts * 16, width // pieces), BF16),
            pltpu.VMEM((experts * 16, width // pieces), BF16),
            pltpu.VMEM((experts * 16, width // pieces), BF16),
            pltpu.VMEM((rows, main), BF16),
            pltpu.VMEM((pieces * rows, experts * 16), BF16),
            pltpu.SemaphoreType.DMA((N_COPIES,)),
            pltpu.SemaphoreType.DMA((N_COPIES,)),
            pltpu.SemaphoreType.DMA((6,)),
            pltpu.SemaphoreType.REGULAR,
            pltpu.SemaphoreType.REGULAR,
            pltpu.SemaphoreType.REGULAR,
        ],
        compiler_params=pltpu.CompilerParams(
            collective_id=0, has_side_effects=True, vmem_limit_bytes=64 * 2**20
        ),
        name="experts_backward",
    )(
        expert_ids.T,
        route_probs.T,
        grad_out,
        tokens,
        jnp.asarray(lmap),
        jnp.asarray(fold, BF16),
        jnp.asarray(unfold, BF16),
        w3.reshape(3 * hidden, width),
        w3,
        pre,
    )
    return gt, jnp.transpose(dw, (2, 0, 1))[None]


def solution(mesh):
    in_specs = (
        P(("fsdp", "exp"), None),
        P(("fsdp", "exp"), None),
        P(("fsdp", "exp"), None),
        P(("fsdp", "exp"), None),
        P("exp", None, None, "fsdp"),
        P("exp", None, None, "fsdp"),
    )
    out_specs = (P(("fsdp", "exp"), None), P("exp", None, None, "fsdp"))
    return jax.shard_map(
        on_device, mesh=mesh, in_specs=in_specs, out_specs=out_specs, check_vma=False
    )
```

```python
import functools

import jax
import jax.numpy as jnp
import numpy as np
from jax import lax
from jax.experimental import pallas as pl
from jax.experimental.pallas import tpu as pltpu
from jax.sharding import PartitionSpec as P

MESH = pl.DeviceIdType.MESH
BF16 = jnp.bfloat16
F32 = jnp.float32
SIDE = 4
N_COPIES = 128


def round_up(value, unit):
    return -(-value // unit) * unit


def chunk_of(width):
    return 512 if width % 512 == 0 else 128


def dot(left, right, dims):
    return lax.dot_general(left, right, (dims, ((), ())), preferred_element_type=F32)


def rows_of(start, size):
    return pl.ds(pl.multiple_of(start, 16), size)


def cols_of(start, size):
    return pl.ds(pl.multiple_of(start, 128), size)


def kernel(
    cap,
    pieces,
    ids_ref,
    probs_ref,
    gout_ref,
    tok_ref,
    lmap_ref,
    fold_ref,
    unfold_ref,
    w_hbm,
    w3_hbm,
    pre_hbm,
    gt_ref,
    dw_hbm,
    g_buf,
    x_buf,
    w13,
    w2,
    pre,
    dgt,
    dg,
    sct,
    acc,
    stage,
    xmain,
    gmain,
    dxr,
    gext,
    gext_got,
    rext,
    rext_got,
    xext,
    xext_got,
    home,
    home_ext,
    send_sem,
    recv_sem,
    local_sem,
    credit_a,
    credit_b,
    credit_z,
):
    f = lax.axis_index("fsdp")
    e = lax.axis_index("exp")
    experts = lax.axis_size("exp")
    core = e % 2
    q = core * (f % SIDE) + (1 - core) * (f // SIDE)
    p = core * (f // SIDE) + (1 - core) * (f % SIDE)
    tokens, width = gout_ref.shape
    half = width // 2
    low, high = pl.ds(0, half), pl.ds(half, half)
    nc = chunk_of(width)
    steps = width // nc
    mb = cap // 16 * 16
    xb = cap - mb
    main = experts * mb
    rb = experts * cap
    rows = SIDE * rb
    rp = g_buf.shape[0]
    h2 = w13.shape[0] // SIDE
    h = h2 // 2
    hp = sct.shape[0] // SIDE
    piece = width // pieces

    def dev_at(pp, qq):
        return (SIDE * (core * pp + (1 - core) * qq) + core * qq + (1 - core) * pp, e)

    def dev_p(d):
        return dev_at((p + d) % SIDE, q)

    def dev_q(d):
        return dev_at(p, (q + d) % SIDE)

    def dev_e(d):
        return (f, (e + d) % experts)

    count = [0]

    def rcopy(src, dst, dev):
        i = count[0]
        count[0] += 1
        c = pltpu.make_async_remote_copy(
            src_ref=src,
            dst_ref=dst,
            send_sem=send_sem.at[i],
            recv_sem=recv_sem.at[i],
            device_id=dev,
            device_id_type=MESH,
        )
        c.start()
        return c

    def signal(sem, devs):
        for dev in devs:
            pl.semaphore_signal(sem, inc=1, device_id=dev, device_id_type=MESH)

    barrier = pltpu.get_barrier_semaphore()
    peers = [dev_p(d) for d in (1, 2, 3)] + [dev_q(d) for d in (1, 2, 3)]
    peers += [dev_e(d) for d in range(1, experts)]
    signal(barrier, peers)
    pl.semaphore_wait(barrier, len(peers))

    def view(ref, where, cols):
        return ref.at[where, :, cols] if len(ref.shape) == 3 else ref.at[where, cols]

    def ring_start(src, buf, off, pos, dev):
        return [
            rcopy(src.at[:, cols], view(buf, off(pos), cols), dev(d))
            for d, cols in ((1, low), (3, high), (1, high), (3, low))
        ]

    def ring_forward(first, buf, off, pos, dev):
        first[0].wait_recv()
        part = view(buf, off((pos + 3) % SIDE), low)
        up = rcopy(part, part, dev(1))
        first[1].wait_recv()
        part = view(buf, off((pos + 1) % SIDE), high)
        down = rcopy(part, part, dev(3))
        return [up, down]

    def wait_recv(copies):
        for c in copies:
            c.wait_recv()

    def wait_send(copies):
        for c in copies:
            c.wait_send()

    w2_off = lambda j: j
    w13_off = lambda j: rows_of(h2 * j, h2)
    row_off = lambda b: rows_of(rb * b, rb)
    ext_off = lambda b: rows_of(rb * b + main, 16)
    w13_src = w_hbm.at[pl.ds(0, h2)]
    my_pre = pl.ds(pl.multiple_of(q * rp, 128), rp)

    w2_copies = ring_start(w3_hbm.at[2], w2, w2_off, q, dev_q)
    w13_copies = ring_start(w13_src, w13, w13_off, q, dev_q)
    strip = pre_hbm.shape[2] // 2
    local = [
        pltpu.make_async_copy(
            pre_hbm.at[i % 2, :, pl.ds(i // 2 * strip, strip)],
            stage.at[i, :, pl.ds(0, strip)],
            local_sem.at[i],
        )
        for i in range(4)
    ]
    local += [
        pltpu.make_async_copy(w3_hbm.at[2], w2.at[w2_off(q)], local_sem.at[4]),
        pltpu.make_async_copy(w13_src, w13.at[w13_off(q)], local_sem.at[5]),
    ]
    for c in local:
        c.start()

    ids = ids_ref[...]
    probs = probs_ref[...].astype(F32)
    kinds = lax.broadcasted_iota(jnp.int32, (experts, tokens), 0)
    hit = [(kinds == ids[k : k + 1, :]).astype(F32) for k in (0, 1)]
    earlier = (
        lax.broadcasted_iota(jnp.int32, (tokens, tokens), 0)
        < lax.broadcasted_iota(jnp.int32, (tokens, tokens), 1)
    ).astype(F32).astype(BF16)
    before = dot((hit[0] + hit[1]).astype(BF16), earlier, ((1,), (0,)))
    at_main, at_ext = [], []
    for k in (0, 1):
        own = ids[k : k + 1, :]
        slot = jnp.sum(before * hit[k], axis=0, keepdims=True).astype(jnp.int32)
        inside = slot < mb
        at_main.append(jnp.where(inside, mb * own + slot, -4096))
        at_ext.append(jnp.where(inside, -4096, 16 * own + pieces * (slot - mb)))

    def one_hot(size, where):
        line = lax.broadcasted_iota(jnp.int32, (size, tokens), 0)
        return [(line == w).astype(F32) for w in where]

    def dispatch(source, weights, big, small):
        pick = one_hot(main, at_main)
        if weights is None:
            home[...] = jnp.transpose(pick[0] + pick[1]).astype(BF16)
            pick = (pick[0] + pick[1]).astype(BF16)
        else:
            pick = (pick[0] * weights[0:1, :] + pick[1] * weights[1:2, :]).astype(BF16)

        def pick_step(n, _):
            cols = cols_of(n * nc, nc)
            big[:, cols] = dot(pick, source[:, cols], ((1,), (0,))).astype(BF16)
            return 0

        lax.fori_loop(0, steps, pick_step, 0)
        folded = jnp.zeros((experts * 16, piece), F32)
        for j in range(pieces):
            pick = one_hot(experts * 16, [w + j for w in at_ext])
            if weights is None:
                pick = pick[0] + pick[1]
                home_ext[pl.ds(j * tokens, tokens), :] = jnp.transpose(pick).astype(BF16)
            else:
                pick = pick[0] * weights[0:1, :] + pick[1] * weights[1:2, :]
            folded += dot(pick.astype(BF16), source[:, pl.ds(j * piece, piece)], ((1,), (0,)))
        small[...] = folded.astype(BF16)

    my_slots = rows_of(rb * p + mb * e, mb)

    def exchange(big, small, buf, small_got):
        copies = []
        for d in range(1, experts):
            to = (e + d) % experts
            there = p if d % 2 == 0 else q
            copies += [
                rcopy(
                    big.at[rows_of(mb * to, mb)],
                    buf.at[rows_of(rb * there + mb * e, mb)],
                    dev_e(d),
                ),
                rcopy(small.at[rows_of(16 * to, 16)], small_got.at[rows_of(16 * e, 16)], dev_e(d)),
            ]
        buf[my_slots, :] = big[rows_of(mb * e, mb), :]
        small_got[rows_of(16 * e, 16), :] = small[rows_of(16 * e, 16), :]
        return copies

    def unfold(buf, small_got):
        for j in range(pieces):
            buf[ext_off(p), pl.ds(j * piece, piece)] = dot(
                unfold_ref[pl.ds(16 * j, 16), :], small_got[...], ((1,), (0,))
            ).astype(BF16)

    dispatch(gout_ref, probs, gmain, gext)
    g_sent = exchange(gmain, gext, g_buf, gext_got)
    dispatch(tok_ref, None, xmain, xext)
    blank = pl.ds(rows, rp - rows)
    g_buf[blank, :] = jnp.zeros((rp - rows, width), BF16)
    x_buf[blank, :] = jnp.zeros((rp - rows, width), BF16)

    for c in local[:4]:
        c.wait()
    span = rp // 3
    line = lax.broadcasted_iota(jnp.int32, (span, span), 0)
    lane = lax.broadcasted_iota(jnp.int32, (span, span), 1)

    def regroup(to, _):
        for n in range(3):
            total = [jnp.zeros((h, span), F32)] * 2
            source = lmap_ref[0:1, pl.ds(n * span, span)]
            for b in (n, n + 1):
                block = core * (SIDE * b + to) + (1 - core) * (SIDE * to + b)
                start = rb * (block % 8)
                window = cols_of(start // 128 * 128, span)
                at = lane + (n * span - rb * b)
                match = (at >= 0) & (at < rb) & (line - start % 128 == source)
                match = match.astype(F32).astype(BF16)
                total = [
                    total[i] + dot(stage[block // 8 * 2 + i, :, window], match, ((1,), (0,)))
                    for i in (0, 1)
                ]
            both = jnp.concatenate(total, 0).astype(BF16)
            dgt[rows_of(h2 * to, h2), pl.ds(n * span, span)] = both
        return 0

    lax.fori_loop(0, SIDE, regroup, 0)
    pre_copies = [
        rcopy(dgt.at[rows_of(h2 * ((q + d) % SIDE), h2)], pre.at[:, my_pre], dev_q(d))
        for d in (1, 2, 3)
    ]
    own_pre = pltpu.make_async_copy(dgt.at[rows_of(h2 * q, h2)], pre.at[:, my_pre], local_sem.at[0])
    own_pre.start()

    w2_copies += ring_forward(w2_copies, w2, w2_off, q, dev_q)

    wait_recv(g_sent)
    unfold(g_buf, gext_got)
    g_copies = ring_start(g_buf.at[row_off(p)], g_buf, row_off, p, dev_p)

    x_sent = exchange(xmain, xext, x_buf, xext_got)
    w13_copies += ring_forward(w13_copies, w13, w13_off, q, dev_q)
    g_copies += ring_forward(g_copies, g_buf, row_off, p, dev_p)
    wait_recv(x_sent)
    unfold(x_buf, xext_got)
    x_copies = ring_start(x_buf.at[row_off(p)], x_buf, row_off, p, dev_p)

    wait_send(g_sent)
    signal(credit_z, [dev_e(d) for d in range(1, experts)])
    local[4].wait()
    local[5].wait()
    wait_recv(w2_copies[2:])
    wait_recv(g_copies[2:])

    acc[...] = jnp.zeros_like(acc)

    def back_step(n, _):
        cols = cols_of(n * nc, nc)
        rows_g = g_buf[:, cols]
        for j in range(SIDE):
            acc[pl.ds(h * j, h), :] += dot(w2[j, :, cols], rows_g, ((1,), (1,)))
        return 0

    lax.fori_loop(0, steps, back_step, 0)
    wait_recv(pre_copies)
    wait_send(pre_copies)
    own_pre.wait()

    def activate(i, _):
        j, c = i // (rp // 128), i % (rp // 128)
        lanes = cols_of(c * 128, 128)
        saved = pre[:, cols_of(j * rp + c * 128, 128)].astype(F32)
        back = acc[pl.ds(pl.multiple_of(h * j, 8), h), lanes]
        a, b = saved[:h], saved[h:]
        sig = jax.nn.sigmoid(a)
        act = a * sig
        d_gate = back * b * sig * (1.0 + a * (1.0 - sig))
        d_up = back * act
        dgt[rows_of(h2 * j, h2), lanes] = jnp.concatenate([d_gate, d_up], 0).astype(BF16)
        scaled = jnp.concatenate([act * b, jnp.zeros((hp - h, 128), F32)], 0)
        sct[rows_of(hp * j, hp), lanes] = scaled.astype(BF16)
        return 0

    lax.fori_loop(0, SIDE * (rp // 128), activate, 0)

    wait_send(w2_copies)
    signal(credit_a, [dev_q(1), dev_q(3)])

    def send_far(part, off, pos, dst, dev):
        far = off((pos + 2) % SIDE)
        return [
            rcopy(view(part, far, low), dst.at[:, low], dev(1)),
            rcopy(view(part, far, high), dst.at[:, high], dev(3)),
        ]

    def send_near_direct(part, off, pos, dst, dev):
        return [
            rcopy(view(part, off((pos + 1) % SIDE), high), dst[0].at[:, high], dev(1)),
            rcopy(view(part, off((pos + 3) % SIDE), low), dst[1].at[:, low], dev(3)),
        ]

    def add_into(part, where, others, start, size, out=None):
        ac = 256 if half % 256 == 0 else 128

        def add_step(n, _):
            cols = cols_of(start + n * ac, ac)
            mine = view(part, where, cols)
            total = mine[...].astype(F32)
            for ref in others:
                total = total + ref[:, cols].astype(F32)
            if out is None:
                mine[...] = total.astype(BF16)
            else:
                for i in (0, 1):
                    out[i][:, cols] = total[h * i : h * (i + 1)].astype(BF16)
            return 0

        lax.fori_loop(0, size // ac, add_step, 0)

    def send_near_added(far, part, off, pos, got, dst, dev):
        far[0].wait_recv()
        where = off((pos + 1) % SIDE)
        add_into(part, where, [got], 0, half)
        up = rcopy(view(part, where, low), dst[0].at[:, low], dev(1))
        far[1].wait_recv()
        where = off((pos + 3) % SIDE)
        add_into(part, where, [got], half, half)
        down = rcopy(view(part, where, high), dst[1].at[:, high], dev(3))
        return [up, down]

    wait_send(x_sent)

    def dw2_step(n, _):
        cols = cols_of(n * nc, nc)
        part = dot(sct[...], g_buf[:, cols], ((1,), (0,)))
        for j in range(SIDE):
            stage[j, :, cols] = part[hp * j : hp * j + h].astype(BF16)
        return 0

    lax.fori_loop(0, steps, dw2_step, 0)
    pl.semaphore_wait(credit_a, 2)
    dw2_near = [w2.at[1], w2.at[2]]
    dw2_far_got = w2.at[0]
    dw2_far = send_far(stage, w2_off, q, dw2_far_got, dev_q)
    x_copies += ring_forward(x_copies, x_buf, row_off, p, dev_p)

    def flip(c, _):
        lanes = cols_of(c * 128, 128)
        dg[rows_of(c * 128, 128), :] = jnp.transpose(dgt[:, lanes])
        return 0

    lax.fori_loop(0, rp // 128, flip, 0)

    wait_send(g_copies)
    wait_recv(w13_copies[2:])

    def dx_block(d):
        b = (p + d) % SIDE

        def dx_step(n, _):
            cols = cols_of(n * nc, nc)
            g_buf[row_off(b), cols] = dot(dg[row_off(b), :], w13[:, cols], ((1,), (0,))).astype(BF16)
            return 0

        lax.fori_loop(0, steps, dx_step, 0)

    dx_far_got = dxr.at[pl.ds(0, rb), pl.ds(0, width)]
    dx_near = [dxr.at[pl.ds(rb * i, rb), pl.ds(0, width)] for i in (1, 2)]
    dx_block(2)
    dx_far = send_far(g_buf, row_off, p, dx_far_got, dev_p)
    dx_block(1)
    dx_block(3)
    dx_mid = send_near_direct(g_buf, row_off, p, dx_near, dev_p)
    dx_block(0)
    dx_mid += send_near_added(dx_far, g_buf, row_off, p, dx_far_got, dx_near, dev_p)
    dw2_mid = send_near_direct(stage, w2_off, q, dw2_near, dev_q)
    dw2_mid += send_near_added(dw2_far, stage, w2_off, q, dw2_far_got, dw2_near, dev_q)

    wait_recv(x_copies[2:])
    wait_send(w13_copies)

    def dw13_block(d):
        j = (q + d) % SIDE

        def dw13_step(n, _):
            cols = cols_of(n * nc, nc)
            w13[w13_off(j), cols] = dot(
                dgt[w13_off(j), :], x_buf[:, cols], ((1,), (0,))
            ).astype(BF16)
            return 0

        lax.fori_loop(0, steps, dw13_step, 0)

    dw13_far_got = pre.at[:, pl.ds(0, width)]
    dw13_near = [x_buf.at[pl.ds(0, h2)], x_buf.at[pl.ds(h2, h2)]]
    dw13_block(2)
    dw13_far = send_far(w13, w13_off, q, dw13_far_got, dev_q)
    dw13_block(1)
    dw13_block(3)
    dw13_block(0)
    wait_send(x_copies)
    signal(credit_b, [dev_q(1), dev_q(3)])
    pl.semaphore_wait(credit_b, 2)
    dw13_mid = send_near_direct(w13, w13_off, q, dw13_near, dev_q)
    wait_recv(dx_mid[1:3])
    add_into(g_buf, row_off(p), dx_near, 0, half)
    wait_recv([dx_mid[0], dx_mid[3]])
    add_into(g_buf, row_off(p), dx_near, half, half)
    folded = jnp.zeros((experts * 16, piece), F32)
    for j in range(pieces):
        folded += dot(
            fold_ref[pl.ds(j * experts * 16, experts * 16), :],
            g_buf[ext_off(p), pl.ds(j * piece, piece)],
            ((1,), (0,)),
        )
    rext[...] = folded.astype(BF16)
    pl.semaphore_wait(credit_z, experts - 1)
    ret = []
    for d in range(1, experts):
        to = (e + d) % experts
        ret.append(
            rcopy(
                g_buf.at[rows_of(rb * p + mb * to, mb)], gmain.at[rows_of(mb * e, mb)], dev_e(d)
            )
        )
        ret.append(
            rcopy(rext.at[rows_of(16 * to, 16)], rext_got.at[rows_of(16 * e, 16)], dev_e(d))
        )
    gmain[rows_of(mb * e, mb), :] = g_buf[my_slots, :]
    rext_got[rows_of(16 * e, 16), :] = rext[rows_of(16 * e, 16), :]

    dw13_mid += send_near_added(dw13_far, w13, w13_off, q, dw13_far_got, dw13_near, dev_q)

    wait_recv(dw2_mid)
    add_into(stage, w2_off(q), dw2_near, 0, width)
    full = pl.ds(0, width)
    outs = [pltpu.make_async_copy(stage.at[q, :, full], dw_hbm.at[2], local_sem.at[2])]
    outs[0].start()

    wait_recv(ret)
    for j in range(pieces):
        cols = pl.ds(j * piece, piece)
        total = dot(home[...], gmain[:, cols], ((1,), (0,)))
        total += dot(home_ext[pl.ds(j * tokens, tokens), :], rext_got[...], ((1,), (0,)))
        gt_ref[:, cols] = total.astype(BF16)

    wait_send(dw2_far + dw2_mid)
    sums = [stage.at[(q + 1 + i) % SIDE] for i in (0, 1)]
    for part, cols in ((0, low), (1, high)):
        wait_recv(dw13_mid[1:3] if part == 0 else [dw13_mid[0], dw13_mid[3]])
        add_into(w13, w13_off(q), dw13_near, part * half, half, sums)
        for i in (0, 1):
            outs.append(
                pltpu.make_async_copy(
                    sums[i].at[:, cols], dw_hbm.at[i, :, cols], local_sem.at[3 * part + i]
                )
            )
            outs[-1].start()

    wait_send(dx_far + dx_mid + dw13_far + dw13_mid + ret)
    for c in outs:
        c.wait()


def on_device(tokens, grad_out, route_probs, expert_ids, saved_pre, expert_weights):
    rows, width = tokens.shape
    experts = lax.axis_size("exp")
    cap = 17 * rows // (8 * experts)
    mb = cap // 16 * 16
    xb = cap - mb
    main = experts * mb
    rb = experts * cap
    hidden = expert_weights.shape[3]
    hp = round_up(hidden, 16)
    rp = round_up(SIDE * rb + 64, 128)
    strip = saved_pre.shape[1] // 2
    pieces = max(k for k in range(1, 16 // xb + 1) if width % (128 * k) == 0)
    w3 = jnp.transpose(expert_weights[0], (1, 2, 0))
    pre = jnp.transpose(saved_pre[0], (1, 2, 0))

    at = np.arange(rb)
    in_main = at // mb * cap + at % mb
    in_ext = (at - main) // xb * cap + mb + (at - main) % xb
    lmap = np.full((8, rp), -1, np.int32)
    lmap[:, : SIDE * rb] = np.tile(np.where(at < main, in_main, in_ext), SIDE)
    ext = np.arange(16)
    unfold = np.zeros((pieces, 16, experts * 16), np.float32)
    for j in range(pieces):
        unfold[j, ext, 16 * (ext // xb) + pieces * (ext % xb) + j] = 1
    fold = unfold.transpose(0, 2, 1).reshape(pieces * experts * 16, 16)
    unfold = unfold.reshape(pieces * 16, experts * 16)

    vmem = pl.BlockSpec(memory_space=pltpu.VMEM)
    hbm = pl.BlockSpec(memory_space=pl.ANY)
    gt, dw = pl.pallas_call(
        functools.partial(kernel, cap, pieces),
        out_shape=(
            jax.ShapeDtypeStruct((rows, width), BF16),
            jax.ShapeDtypeStruct((3, hidden, width), BF16),
        ),
        in_specs=[vmem] * 7 + [hbm] * 3,
        out_specs=(vmem, hbm),
        scratch_shapes=[
            pltpu.VMEM((rp, width), BF16),
            pltpu.VMEM((rp, width), BF16),
            pltpu.VMEM((SIDE * 2 * hidden, width), BF16),
            pltpu.VMEM((SIDE, hidden, width), BF16),
            pltpu.VMEM((2 * hidden, SIDE * rp), BF16),
            pltpu.VMEM((SIDE * 2 * hidden, rp), BF16),
            pltpu.VMEM((rp, SIDE * 2 * hidden), BF16),
            pltpu.VMEM((SIDE * hp, rp), BF16),
            pltpu.VMEM((SIDE * hidden, rp), F32),
            pltpu.VMEM((SIDE, hidden, max(width, strip)), BF16),
            pltpu.VMEM((main, width), BF16),
            pltpu.VMEM((main, width), BF16),
            pltpu.VMEM((3 * rb, width), BF16),
            pltpu.VMEM((experts * 16, width // pieces), BF16),
            pltpu.VMEM((experts * 16, width // pieces), BF16),
            pltpu.VMEM((experts * 16, width // pieces), BF16),
            pltpu.VMEM((experts * 16, width // pieces), BF16),
            pltpu.VMEM((experts * 16, width // pieces), BF16),
            pltpu.VMEM((experts * 16, width // pieces), BF16),
            pltpu.VMEM((rows, main), BF16),
            pltpu.VMEM((pieces * rows, experts * 16), BF16),
            pltpu.SemaphoreType.DMA((N_COPIES,)),
            pltpu.SemaphoreType.DMA((N_COPIES,)),
            pltpu.SemaphoreType.DMA((6,)),
            pltpu.SemaphoreType.REGULAR,
            pltpu.SemaphoreType.REGULAR,
            pltpu.SemaphoreType.REGULAR,
        ],
        compiler_params=pltpu.CompilerParams(
            collective_id=0, has_side_effects=True, vmem_limit_bytes=64 * 2**20
        ),
        name="experts_backward",
    )(
        expert_ids.T,
        route_probs.T,
        grad_out,
        tokens,
        jnp.asarray(lmap),
        jnp.asarray(fold, BF16),
        jnp.asarray(unfold, BF16),
        w3.reshape(3 * hidden, width),
        w3,
        pre,
    )
    return gt, jnp.transpose(dw, (2, 0, 1))[None]


def solution(mesh):
    in_specs = (
        P(("fsdp", "exp"), None),
        P(("fsdp", "exp"), None),
        P(("fsdp", "exp"), None),
        P(("fsdp", "exp"), None),
        P("exp", None, None, "fsdp"),
        P("exp", None, None, "fsdp"),
    )
    out_specs = (P(("fsdp", "exp"), None), P("exp", None, None, "fsdp"))
    return jax.shard_map(
        on_device, mesh=mesh, in_specs=in_specs, out_specs=out_specs, check_vma=False
    )
```
